256 devices in a mesh: ctx: 64 (over x, z, core), tp: 4 (over y).
Axes of the slice: x: 4, y: 4, z: 8, core: 2. Of those that a mesh axis runs over, the one named last changes fastest.
Arguments:
- tokens: bfloat16 [24576, 5120], P('ctx', 'tp'), may hold values from -6 to 6
- input_gain: float32 [5120], replicated, may hold values from 0.5 to 1.5
- w_query: bfloat16 [5120, 2560], P('ctx', 'tp'), may hold values from -0.078125 to 0.078125
- w_key: bfloat16 [5120, 512], P('ctx', 'tp'), may hold values from -0.078125 to 0.078125
- w_value: bfloat16 [5120, 512], P('ctx', 'tp'), may hold values from -0.078125 to 0.078125
- query_bias: float32 [2560], P('tp'), may hold values from -8 to 8
- key_bias: float32 [512], P('tp'), may hold values from -8 to 8
- value_bias: float32 [512], P('tp'), may hold values from -3 to 3
- w_out: bfloat16 [2560, 5120], P('tp', 'ctx'), may hold values from -0.125 to 0.125
- final_gain: float32 [5120], P('tp'), may hold values from 0.5 to 1.5
- critic_head: float32 [5120], P('tp'), may hold values from -0.078125 to 0.078125
- critic_bias: float32 [1], replicated, may hold values from -1 to 1
- rewards: int32 [24576], P('ctx'), may hold values from -4 to 4
- turn_ends: int32 [24576], P('ctx'), may hold values 0 or 1
- episode_done: int32 [24576], P('ctx'), may hold values 0 or 1
Outputs:
- residual_stream: bfloat16 [24576, 5120], P('ctx', 'tp')
- values: float32 [24576], P('ctx')
- advantages: float32 [24576], P('ctx')
The draws below stay inside these ranges and needn't reach their ends.
All inputs are finite; a program needn't handle non-finite values. No bound on the sum of `turn_ends` or of `episode_done` on one device may be relied on, other than what follows from the above.
Results may differ from the reference program's by a relative error of at most 0.013.
The reference program's roundings to bfloat16 on the way count: a program that leaves them out, or rounds other values in their place, can miss the bound.
Values may be sent and summed in bfloat16 or wider, within the bound.
No kernel may reach another device: no remote copies, remote signals or barrier semaphores. Data moves between devices by JAX's collectives and lax.ppermute only.
A program may use at most 64 MiB of HBM per device.

```python
import jax
import jax.numpy as jnp
from jax import lax

D = 5120
HQ = 20
HK = 4
HD = 128
TOK_DEV = 384
TOKENS = 24576
N_CTX = 64


def drawn_bias(key, heads, scale):
    key = jax.random.fold_in(key, scale)
    second = jax.random.fold_in(key, 1)
    drawn = 0.5 * jax.random.normal(second, (heads, HD), jnp.float32)
    return jnp.clip(drawn, -8.0, 8.0).reshape(heads * HD)


def draw_query_bias(key, part):
    return drawn_bias(key, HQ, 11)


def draw_key_bias(key, part):
    return drawn_bias(key, HK, 23)


def plant(array, stream_key, least, top_value):
    longest = array.shape.index(max(array.shape))
    spots = []
    for shift in (0, 1):
        where = [jax.random.randint(jax.random.fold_in(stream_key, axis), (), 0, length) for axis, length in enumerate(array.shape)]
        where[longest] = (where[longest] + shift) % array.shape[longest]
        spots.append(tuple(where))
    return array.at[spots[0]].set(least).at[spots[1]].set(top_value)


def shard_levels(key, extent, cuts, low, high):
    gain, own = 1.0, jax.random.fold_in(key, 6)
    for axis_at, parts in cuts:
        heights = jnp.exp(jax.random.uniform(jax.random.fold_in(own, axis_at), (parts,), jnp.float32, low / len(cuts), high / len(cuts)))
        gain = gain * jnp.repeat(heights, extent[axis_at] // parts).reshape([-1 if axis == axis_at else 1 for axis in range(len(extent))])
    return gain


def gaussian(rng, extent, deviation, limit, pieces=(), held_as=jnp.bfloat16):
    values = deviation * jax.random.normal(rng, extent, jnp.float32)
    if pieces:
        values = values * shard_levels(rng, extent, pieces, -0.22, 0.18)
    return jnp.clip(values, -limit, limit).astype(held_as)


def setup_inputs(seed: int = 0) -> dict:
    seeds = jax.random.split(jax.random.key(seed), 16)
    return {
        "tokens": gaussian(seeds[0], (TOKENS, D), 1.0, 6.0, ((0, 64), (1, 4))),
        "input_gain": jnp.clip(1.0 + 0.1 * jax.random.normal(seeds[1], (D,), jnp.float32), 0.5, 1.5),
        "w_query": gaussian(seeds[2], (D, HQ * HD), D ** -0.5, 0.078125, ((0, 64), (1, 4))),
        "w_key": gaussian(seeds[3], (D, HK * HD), D ** -0.5, 0.078125, ((0, 64), (1, 4))),
        "w_value": gaussian(seeds[4], (D, HK * HD), D ** -0.5, 0.078125, ((0, 64), (1, 4))),
        "query_bias": draw_query_bias(jax.random.fold_in(seeds[15], 71), 0),
        "key_bias": draw_key_bias(jax.random.fold_in(seeds[15], 71), 0),
        "value_bias": gaussian(seeds[7], (HK * HD,), 0.5, 3.0, ((0, 4),), jnp.float32),
        "w_out": gaussian(seeds[8], (HQ * HD, D), (HQ * HD) ** -0.5, 0.125, ((0, 4), (1, 64))),
        "final_gain": jnp.clip(1.0 + 0.1 * jax.random.normal(seeds[9], (D,), jnp.float32), 0.5, 1.5),
        "critic_head": gaussian(seeds[10], (D,), D ** -0.5, 0.078125, ((0, 4),), jnp.float32),
        "critic_bias": jnp.clip(jax.random.uniform(seeds[11], (1,), jnp.float32, -1.0, 1.0), -1.0, 1.0),
        "rewards": plant(jax.random.randint(seeds[12], (TOKENS,), -4, 5), jax.random.fold_in(seeds[12], 1), -4, 4).astype(jnp.int32),
        "turn_ends": plant((jax.random.randint(seeds[13], (TOKENS,), 0, TOK_DEV) < 4).astype(jnp.int32), jax.random.fold_in(seeds[13], 1), 0, 1),
        "episode_done": plant((jax.random.randint(seeds[14], (TOKENS,), 0, 8 * TOK_DEV) < 1).astype(jnp.int32), jax.random.fold_in(seeds[14], 1), 0, 1),
    }


EPS = 1e-06
GAMMA = 0.99
LAMBDA = 0.95
ROPE_BASE = 1000000.0
REWARD_SCALE = 0.25

def rotary(values, positions):
    half = values.shape[-1] // 2
    steps = jnp.arange(half).astype(jnp.float32)
    inverse = 1.0 / ROPE_BASE ** (steps * 2.0 / values.shape[-1])
    angle = positions.astype(jnp.float32)[:, None] * inverse[None, :]
    cosine = jnp.cos(angle)[:, None, :]
    sine = jnp.sin(angle)[:, None, :]
    first = values[..., :half]
    second = values[..., half:]
    return jnp.concatenate([first * cosine - second * sine, second * cosine + first * sine], axis=-1)

def reference(tokens, input_gain, w_query, w_key, w_value, query_bias, key_bias, value_bias, w_out, final_gain, critic_head, critic_bias, rewards, turn_ends, episode_done):
    xfull = tokens.astype(jnp.float32)
    normed = (xfull * lax.rsqrt(lax.optimization_barrier(jnp.mean(xfull * xfull, axis=-1, keepdims=True)) + EPS) * input_gain).astype(jnp.bfloat16)
    positions = jnp.arange(TOKENS).astype(jnp.int32)
    query = jnp.dot(normed, w_query, preferred_element_type=jnp.float32) + query_bias
    keys = jnp.dot(normed, w_key, preferred_element_type=jnp.float32) + key_bias
    vals = jnp.dot(normed, w_value, preferred_element_type=jnp.float32) + value_bias
    group = HQ // HK
    query = rotary(query.reshape(TOKENS, HQ, HD), positions).astype(jnp.bfloat16).reshape(TOKENS, HK, group, HD)
    keys = rotary(keys.reshape(TOKENS, HK, HD), positions).astype(jnp.bfloat16)
    vals = vals.astype(jnp.bfloat16).reshape(TOKENS, HK, HD)
    anchor_keys = keys[:TOK_DEV].astype(jnp.float32)
    anchor_vals = vals[:TOK_DEV].astype(jnp.float32)
    scale = HD ** (-0.5)
    causal = jnp.arange(TOK_DEV)[:, None] >= jnp.arange(TOK_DEV)[None, :]

    def one_block(block):
        start = (block * TOK_DEV).astype(jnp.int32)
        block_q = lax.dynamic_slice_in_dim(query, start, TOK_DEV, 0).astype(jnp.float32)
        block_k = lax.dynamic_slice_in_dim(keys, start, TOK_DEV, 0).astype(jnp.float32)
        block_v = lax.dynamic_slice_in_dim(vals, start, TOK_DEV, 0).astype(jnp.float32)
        s_anchor = jnp.einsum('tkgd,skd->kgts', block_q, anchor_keys) * scale
        s_anchor = jnp.where(block > 0, s_anchor, -jnp.inf)
        s_local = jnp.einsum('tkgd,skd->kgts', block_q, block_k) * scale
        s_local = jnp.where(causal, s_local, -jnp.inf)
        peak = jnp.maximum(lax.optimization_barrier(jnp.max(s_anchor, axis=-1)), lax.optimization_barrier(jnp.max(s_local, axis=-1)))
        p_anchor = jnp.exp(s_anchor - peak[..., None])
        p_local = jnp.exp(s_local - peak[..., None])
        total = lax.optimization_barrier(jnp.sum(p_anchor, axis=-1)) + lax.optimization_barrier(jnp.sum(p_local, axis=-1))
        mixed = jnp.einsum('kgts,skd->tkgd', p_anchor.astype(jnp.bfloat16).astype(jnp.float32), anchor_vals)
        mixed = mixed + jnp.einsum('kgts,skd->tkgd', p_local.astype(jnp.bfloat16).astype(jnp.float32), block_v)
        mixed = mixed / jnp.transpose(total, (2, 0, 1))[..., None]
        return mixed.astype(jnp.bfloat16).reshape(TOK_DEV, HQ * HD)
    attended = lax.map(one_block, jnp.arange(N_CTX).astype(jnp.int32)).reshape(TOKENS, HQ * HD)
    resid = xfull + jnp.dot(attended, w_out, preferred_element_type=jnp.float32)
    residual_stream = resid.astype(jnp.bfloat16)
    values = lax.optimization_barrier(jnp.sum(resid * final_gain * critic_head, axis=-1)) * lax.rsqrt(lax.optimization_barrier(jnp.mean(resid * resid, axis=-1)) + EPS) + critic_bias[0]
    ends = jnp.maximum(turn_ends, episode_done)
    discount = jnp.where(ends > 0, GAMMA, 1.0).astype(jnp.float32)
    trace = jnp.where(ends > 0, LAMBDA, 1.0).astype(jnp.float32)
    keep = (1 - episode_done).astype(jnp.float32)
    reward = REWARD_SCALE * (rewards * ends).astype(jnp.float32)
    next_values = jnp.concatenate([values[1:], jnp.zeros((1,), jnp.float32)])
    delta = reward + discount * keep * next_values - values
    factor = discount * trace * keep

    def backward(carry, item):
        term, decay = item
        carry = term + decay * carry
        return (carry, carry)
    start_carry = jnp.zeros((), jnp.float32)
    unused, advantages = lax.scan(backward, start_carry, (delta, factor), reverse=True)
    return (residual_stream, values, advantages)
```

```python
import jax
import jax.numpy as jnp
from jax import lax
from jax.experimental import pallas as pl
from jax.experimental.pallas import tpu as pltpu
from jax.sharding import PartitionSpec as P

D = 5120
HD = 128
HALF = HD // 2
GROUP = 5
QW = GROUP * HD

EPS = 1e-06
GAMMA = 0.99
LAMBDA = 0.95
ROPE_BASE = 1000000.0
REWARD_SCALE = 0.25

X, Z, C, T = 4, 8, 2, 4
ROWS = 384
PIECE = D // T
MIB = 1 << 20

F32 = jnp.float32
BF16 = jnp.bfloat16


def place(x, z, c):
    return (x * Z + z) * C + c


def shift_tp(block, distance):
    return lax.ppermute(block, "tp", [(i, (i + distance) % T) for i in range(T)])


def ring_tp(block):
    half = block.shape[0] // 2
    below = shift_tp(block, 1)
    above = shift_tp(block, -1)
    first = shift_tp(below[:half], 1)
    second = shift_tp(above[half:], -1)
    return block, below, above, first, second


def params(mib=40):
    return pltpu.CompilerParams(vmem_limit_bytes=mib * MIB)


def project_kernel(
    order, own, below, above, first, second, gain, w_q, w_kv, bias, cosine, sine, q_out, kv_out, scale, acc
):
    step = pl.program_id(0)
    half = first.shape[0]

    @pl.when(step == 0)
    def _():
        def squares(ref):
            x = ref[...].astype(F32)
            return jnp.sum(x * x, axis=-1, keepdims=True)

        far = jnp.concatenate([squares(first), squares(second)], axis=0)
        mean = (squares(own) + squares(below) + squares(above) + far) / D
        scale[...] = lax.rsqrt(mean + EPS)
        acc[...] = jnp.zeros_like(acc)

    def add(x, rows):
        normed = (x.astype(F32) * scale[rows, :] * gain[0]).astype(BF16)
        acc[rows, :QW] += jnp.dot(normed, w_q[...], preferred_element_type=F32)
        acc[rows, QW:] += jnp.dot(normed, w_kv[...], preferred_element_type=F32)

    everything = pl.ds(0, ROWS)
    for at, ref in enumerate((own, below, above)):

        @pl.when(step == at)
        def _(ref=ref):
            add(ref[...], everything)

    @pl.when(step == T - 1)
    def _():
        add(first[...], pl.ds(0, half))
        add(second[...], pl.ds(half, half))

        def rotary(u):
            return u * cosine[...] + pltpu.roll(u, HALF, 1) * sine[...]

        for head in range(GROUP):
            span = slice(head * HD, (head + 1) * HD)
            q_out[:, span] = rotary(acc[:, span] + bias[:, span]).astype(BF16)
        span = slice(QW, QW + HD)
        kv_out[:, :HD] = rotary(acc[:, span] + bias[:, span]).astype(BF16)
        span = slice(QW + HD, QW + 2 * HD)
        kv_out[:, HD:] = (acc[:, span] + bias[:, span]).astype(BF16)


def project(order, pieces, gain, weights, bias, cosine, sine):
    whole = lambda *shape: pl.BlockSpec(shape, lambda k, order: (0,) * len(shape))
    wide = QW + 2 * HD
    grid = pltpu.PrefetchScalarGridSpec(
        num_scalar_prefetch=1,
        grid=(T,),
        in_specs=[
            whole(ROWS, PIECE),
            whole(ROWS, PIECE),
            whole(ROWS, PIECE),
            whole(ROWS // 2, PIECE),
            whole(ROWS // 2, PIECE),
            pl.BlockSpec((1, 1, PIECE), lambda k, order: (order[k], 0, 0)),
            pl.BlockSpec((PIECE, QW), lambda k, order: (order[k], 1)),
            pl.BlockSpec((PIECE, 2 * HD), lambda k, order: (order[k], 5)),
            whole(1, wide),
            whole(ROWS, HD),
            whole(ROWS, HD),
        ],
        out_specs=[whole(ROWS, QW), whole(ROWS, 2 * HD)],
        scratch_shapes=[pltpu.VMEM((ROWS, 1), F32), pltpu.VMEM((ROWS, wide), F32)],
    )
    return pl.pallas_call(
        project_kernel,
        grid_spec=grid,
        out_shape=[
            jax.ShapeDtypeStruct((ROWS, QW), BF16),
            jax.ShapeDtypeStruct((ROWS, 2 * HD), BF16),
        ],
        compiler_params=params(),
        cost_estimate=pl.CostEstimate(
            flops=2 * ROWS * D * wide, bytes_accessed=2 * D * (wide + ROWS), transcendentals=0
        ),
        name="project",
    )(order, *pieces, gain, weights, weights, bias, cosine, sine)


def attend_kernel(index, q, kv, anchor, out, bias):
    keep_anchor = jnp.full((ROWS, ROWS), index[0], jnp.int32) > 0
    row = lax.broadcasted_iota(jnp.int32, (ROWS, ROWS), 0)
    col = lax.broadcasted_iota(jnp.int32, (ROWS, ROWS), 1)
    bias[:, :ROWS] = jnp.where(keep_anchor, 0.0, -jnp.inf)
    bias[:, ROWS:] = jnp.where(row >= col, 0.0, -jnp.inf)
    keys = jnp.concatenate([anchor[:, :HD], kv[:, :HD]], axis=0)
    vals = jnp.concatenate([anchor[:, HD:], kv[:, HD:]], axis=0)
    for head in range(GROUP):
        span = slice(head * HD, (head + 1) * HD)
        scores = lax.dot_general(q[:, span], keys, (((1,), (1,)), ((), ())), preferred_element_type=F32)
        scores = scores * (HD**-0.5) + bias[...]
        peak = jnp.max(scores, axis=-1, keepdims=True)
        weights = jnp.exp(scores - peak)
        total = jnp.sum(weights, axis=-1, keepdims=True)
        mixed = jnp.dot(weights.astype(BF16), vals, preferred_element_type=F32)
        out[:, span] = (mixed / total).astype(BF16)


def attend(index, q, kv, anchor):
    vmem = pl.BlockSpec(memory_space=pltpu.VMEM)
    return pl.pallas_call(
        attend_kernel,
        in_specs=[pl.BlockSpec(memory_space=pltpu.SMEM), vmem, vmem, vmem],
        out_specs=vmem,
        out_shape=jax.ShapeDtypeStruct((ROWS, QW), BF16),
        scratch_shapes=[pltpu.VMEM((ROWS, 2 * ROWS), F32)],
        compiler_params=params(),
        cost_estimate=pl.CostEstimate(
            flops=4 * ROWS * 2 * ROWS * QW, bytes_accessed=4 * ROWS * QW, transcendentals=ROWS * 2 * ROWS * GROUP
        ),
        name="attend",
    )(index, q, kv, anchor)


def times(a, w):
    return lax.dot_general(a, w, (((1,), (1,)), ((), ())), preferred_element_type=F32)


def out_own_kernel(order, tokens, att, w, out):
    out[...] = tokens[...].astype(F32) + times(att[...], w[...])


def out_next_kernel(order, total, below, above, w_below, w_above, out):
    out[...] = total[...] + times(below[...], w_below[...]) + times(above[...], w_above[...])


def out_last_kernel(order, total, first, second, w, gain, head, resid_out, stats_out):
    half = first.shape[0]
    lane = lax.broadcasted_iota(jnp.int32, (half, HD), 1)
    for at, ref in enumerate((first, second)):
        rows = pl.ds(at * half, half)
        resid = total[rows, :] + times(ref[...], w[...])
        resid_out[rows, :] = resid.astype(BF16)
        squares = jnp.sum(resid * resid, axis=-1, keepdims=True)
        products = jnp.sum(resid * gain[...] * head[...], axis=-1, keepdims=True)
        both = jnp.where(lane == 0, squares, products)
        stats_out[at] = both.T[:8, :]


def out_call(kernel, order, operands, weights, extra, out_shape, name, flops):
    vmem = lambda shape: pl.BlockSpec(shape, lambda i, order: (0,) * len(shape))
    w_spec = lambda at: pl.BlockSpec((PIECE, QW), lambda i, order, at=at: (order[at], 0))
    grid = pltpu.PrefetchScalarGridSpec(
        num_scalar_prefetch=1,
        grid=(1,),
        in_specs=[vmem(o.shape) for o in operands] + [w_spec(at) for _, at in weights] + [vmem(e.shape) for e in extra],
        out_specs=jax.tree.map(lambda s: vmem(s.shape), out_shape),
    )
    return pl.pallas_call(
        kernel,
        grid_spec=grid,
        out_shape=out_shape,
        compiler_params=params(),
        cost_estimate=pl.CostEstimate(flops=flops, bytes_accessed=6 * MIB, transcendentals=0),
        name=name,
    )(order, *operands, *(w for w, _ in weights), *extra)


def broadcast_anchor(block):
    here = lax.axis_index("ctx")
    holders = [(0, 0, 0)]
    for dx, dz, dc in ((0, 0, 1), (2, 0, 0), (0, 4, 0), (1, 0, 0), (0, 2, 0), (0, 1, 0)):
        fresh = [((x + dx) % X, (z + dz) % Z, (c + dc) % C) for x, z, c in holders]
        sent = lax.ppermute(block, "ctx", [(place(*a), place(*b)) for a, b in zip(holders, fresh)])
        table = jnp.zeros((X * Z * C,), jnp.bool_).at[jnp.array([place(*b) for b in fresh])].set(True)
        block = jnp.where(table[here], sent, block)
        holders = holders + fresh
    return block


def on_device(
    tokens,
    input_gain,
    w_query,
    w_key,
    w_value,
    query_bias,
    key_bias,
    value_bias,
    w_out,
    final_gain,
    critic_head,
    critic_bias,
    rewards,
    turn_ends,
    episode_done,
):
    index = lax.axis_index("ctx")
    mine = lax.axis_index("tp")
    order = jnp.stack([mine, (mine + 3) % T, (mine + 1) % T, (mine + 2) % T]).astype(jnp.int32)

    corner = [
        (place(x, z, c) * T + y, place(y, z, c) * T + x) for x in range(X) for z in range(Z) for c in range(C) for y in range(T)
    ]
    out_block = lax.ppermute(w_out.T, ("ctx", "tp"), corner)
    weights = lax.all_gather(
        jnp.concatenate([out_block, w_query, w_key, w_value], axis=1), "ctx", axis=0, tiled=True
    )

    pieces = ring_tp(tokens)
    positions = (index * ROWS + jnp.arange(ROWS)).astype(F32)
    steps = jnp.arange(HALF).astype(F32)
    inverse = 1.0 / ROPE_BASE ** (steps * 2.0 / HD)
    angle = positions[:, None] * inverse[None, :]
    cosine, sine = jnp.cos(angle), jnp.sin(angle)
    cosine = jnp.concatenate([cosine, cosine], axis=1)
    sine = jnp.concatenate([-sine, sine], axis=1)
    bias = jnp.concatenate([query_bias, key_bias, value_bias])[None, :]
    query, kv = project(order, pieces, input_gain.reshape(T, 1, PIECE), weights, bias, cosine, sine)

    anchor = broadcast_anchor(kv)
    att = attend(index.astype(jnp.int32)[None], query, kv, anchor)

    own, below, above, first, second = ring_tp(att)
    flops = 2 * ROWS * QW * PIECE
    wide = jax.ShapeDtypeStruct((ROWS, PIECE), F32)
    total = out_call(out_own_kernel, order, [tokens, own], [(weights, 0)], [], wide, "out_own", flops)
    total = out_call(
        out_next_kernel, order, [total, below, above], [(weights, 1), (weights, 2)], [], wide, "out_next", 2 * flops
    )
    residual_stream, stats = out_call(
        out_last_kernel,
        order,
        [total, first, second],
        [(weights, 3)],
        [final_gain[None, :], critic_head[None, :]],
        [jax.ShapeDtypeStruct((ROWS, PIECE), BF16), jax.ShapeDtypeStruct((2, 8, ROWS // 2), F32)],
        "out_last",
        flops,
    )
    stats = lax.psum(jnp.concatenate([stats[0, :2], stats[1, :2]], axis=1), "tp")
    values = stats[1] * lax.rsqrt(stats[0] / D + EPS) + critic_bias[0]

    ends = jnp.maximum(turn_ends, episode_done)
    discount = jnp.where(ends > 0, GAMMA, 1.0).astype(F32) * (1 - episode_done).astype(F32)
    reward = REWARD_SCALE * (rewards * ends).astype(F32)
    decaying = ends * (1 - episode_done)
    zero_int = jnp.zeros((1,), jnp.int32)
    decay_count = jnp.concatenate([zero_int, jnp.cumsum(decaying)])
    done_count = jnp.concatenate([zero_int, jnp.cumsum(episode_done)])
    rate = GAMMA * LAMBDA
    later = jnp.arange(ROWS)[None, :] >= jnp.arange(ROWS)[:, None]
    same_episode = done_count[None, :ROWS] == done_count[:ROWS, None]
    powers = (decay_count[None, :ROWS] - decay_count[:ROWS, None]).astype(F32)
    matrix = jnp.where(later & same_episode, jnp.power(rate, powers), 0.0)
    tail_powers = (decay_count[ROWS] - decay_count[:ROWS]).astype(F32)
    tail = jnp.where(done_count[ROWS] == done_count[:ROWS], jnp.power(rate, tail_powers), 0.0)
    edge = matrix[:, ROWS - 1] * discount[ROWS - 1]

    next_values = jnp.concatenate([values[1:], jnp.zeros((1,), F32)])
    delta = reward + discount * next_values - values
    local = jnp.dot(matrix, delta, precision=lax.Precision.HIGHEST)
    record = jnp.stack([values[0], local[0], tail[0], edge[0]])
    n = lax.axis_size("ctx")
    records = jnp.broadcast_to(jnp.concatenate([record, jnp.zeros((HD - 4,), F32)])[None, :], (n, HD))
    records = lax.all_to_all(records, "ctx", 0, 0, tiled=True)
    after_values = jnp.concatenate([records[1:, 0], jnp.zeros((1,), F32)])
    terms = records[:, 1] + records[:, 3] * after_values
    block = jnp.arange(n)
    between = (block[None, :] > index) & (block[None, :] < block[:, None])
    reach = jnp.prod(jnp.where(between, records[None, :, 2], 1.0), axis=1)
    carry = jnp.sum(jnp.where(block > index, reach * terms, 0.0))
    following = jnp.sum(jnp.where(block == index, after_values, 0.0))
    advantages = local + edge * following + tail * carry
    return (residual_stream, values, advantages)


def solution(mesh):
    in_specs = (
        P("ctx", "tp"),
        P(),
        P("ctx", "tp"),
        P("ctx", "tp"),
        P("ctx", "tp"),
        P("tp"),
        P("tp"),
        P("tp"),
        P("tp", "ctx"),
        P("tp"),
        P("tp"),
        P(),
        P("ctx"),
        P("ctx"),
        P("ctx"),
    )
    out_specs = (P("ctx", "tp"), P("ctx"), P("ctx"))
    return jax.shard_map(
        on_device, mesh=mesh, in_specs=in_specs, out_specs=out_specs, check_vma=False
    )
```

```python
import jax
import jax.numpy as jnp
from jax import lax
from jax.experimental import pallas as pl
from jax.experimental.pallas import tpu as pltpu
from jax.sharding import PartitionSpec as P

D = 5120
HD = 128
HALF = HD // 2
GROUP = 5
QW = GROUP * HD

EPS = 1e-06
GAMMA = 0.99
LAMBDA = 0.95
ROPE_BASE = 1000000.0
REWARD_SCALE = 0.25

X, Z, C, T = 4, 8, 2, 4
ROWS = 384
SHARD = 80
PIECE = D // T
MIB = 1 << 20

F32 = jnp.float32
BF16 = jnp.bfloat16


def place(x, z, c):
    return (x * Z + z) * C + c


def shift_tp(block, distance):
    return lax.ppermute(block, "tp", [(i, (i + distance) % T) for i in range(T)])


def ring_tp(block):
    half = block.shape[0] // 2
    below = shift_tp(block, 1)
    above = shift_tp(block, -1)
    first = shift_tp(below[:half], 1)
    second = shift_tp(above[half:], -1)
    return block, below, above, first, second


def params(mib=40):
    return pltpu.CompilerParams(vmem_limit_bytes=mib * MIB)


def interleave(core, own, other, joined):
    joined[:, pl.ds(core, 1)] = own[...].reshape(own.shape[-3], 1, *own.shape[-2:])
    joined[:, pl.ds(1 - core, 1)] = other[...].reshape(other.shape[-3], 1, *other.shape[-2:])
    return joined[...].reshape(-1, joined.shape[-1])


def turned(u, cosine, sine):
    return u * cosine[...] + pltpu.roll(u, HALF, 1) * sine[...]


def project_kv_kernel(
    order, own, below, above, first, second, gain, w_own, w_other, bias, cosine, sine, normed_out, kv_out, scale, acc, joined
):
    step = pl.program_id(0)
    half = first.shape[0]

    @pl.when(step == 0)
    def _():
        def squares(ref):
            x = ref[...].astype(F32)
            return jnp.sum(x * x, axis=-1, keepdims=True)

        far = jnp.concatenate([squares(first), squares(second)], axis=0)
        mean = (squares(own) + squares(below) + squares(above) + far) / D
        scale[...] = lax.rsqrt(mean + EPS)
        acc[...] = jnp.zeros_like(acc)

    def norm(x, rows):
        normed_out[0, rows, :] = (x.astype(F32) * scale[rows, :] * gain[0]).astype(BF16)

    for at, ref in enumerate((own, below, above)):

        @pl.when(step == at)
        def _(ref=ref):
            norm(ref[...], pl.ds(0, ROWS))

    @pl.when(step == T - 1)
    def _():
        norm(first[...], pl.ds(0, half))
        norm(second[...], pl.ds(half, half))

    w = interleave(order[T], w_own, w_other, joined)
    acc[...] += jnp.dot(normed_out[0], w, preferred_element_type=F32)

    @pl.when(step == T - 1)
    def _():
        kv_out[:, :HD] = turned(acc[:, :HD] + bias[:, :HD], cosine, sine).astype(BF16)
        kv_out[:, HD:] = (acc[:, HD:] + bias[:, HD:]).astype(BF16)


def whole(*shape):
    return pl.BlockSpec(shape, lambda k, order: (0,) * len(shape))


def shard_rows(n):
    return pl.BlockSpec((1, Z, SHARD, n), lambda k, order: (order[k], 0, 0, 0))


def project_kv(order, pieces, gain, w_own, w_other, bias, cosine, sine):
    grid = pltpu.PrefetchScalarGridSpec(
        num_scalar_prefetch=1,
        grid=(T,),
        in_specs=[whole(*piece.shape) for piece in pieces]
        + [
            pl.BlockSpec((1, 1, PIECE), lambda k, order: (order[k], 0, 0)),
            shard_rows(2 * HD),
            shard_rows(2 * HD),
            whole(1, 2 * HD),
            whole(ROWS, HD),
            whole(ROWS, HD),
        ],
        out_specs=[pl.BlockSpec((1, ROWS, PIECE), lambda k, order: (k, 0, 0)), whole(ROWS, 2 * HD)],
        scratch_shapes=[
            pltpu.VMEM((ROWS, 1), F32),
            pltpu.VMEM((ROWS, 2 * HD), F32),
            pltpu.VMEM((Z, C, SHARD, 2 * HD), BF16),
        ],
    )
    return pl.pallas_call(
        project_kv_kernel,
        grid_spec=grid,
        out_shape=[
            jax.ShapeDtypeStruct((T, ROWS, PIECE), BF16),
            jax.ShapeDtypeStruct((ROWS, 2 * HD), BF16),
        ],
        compiler_params=params(),
        cost_estimate=pl.CostEstimate(flops=4 * ROWS * D * HD, bytes_accessed=2 * D * (2 * HD + 2 * ROWS), transcendentals=0),
        name="project_kv",
    )(order, *pieces, gain, w_own, w_other, bias, cosine, sine)


def project_q_kernel(order, normed, w, bias, cosine, sine, q_out, acc):
    step = pl.program_id(0)

    @pl.when(step == 0)
    def _():
        acc[...] = jnp.zeros_like(acc)

    acc[...] += jnp.dot(normed[0], w[...], preferred_element_type=F32)

    @pl.when(step == T - 1)
    def _():
        for head in range(GROUP):
            span = slice(head * HD, (head + 1) * HD)
            q_out[:, span] = turned(acc[:, span] + bias[:, span], cosine, sine).astype(BF16)


def project_q(order, normed, w, bias, cosine, sine):
    grid = pltpu.PrefetchScalarGridSpec(
        num_scalar_prefetch=1,
        grid=(T,),
        in_specs=[
            pl.BlockSpec((1, ROWS, PIECE), lambda k, order: (k, 0, 0)),
            pl.BlockSpec((PIECE, QW), lambda k, order: (order[k], 1)),
            whole(1, QW),
            whole(ROWS, HD),
            whole(ROWS, HD),
        ],
        out_specs=whole(ROWS, QW),
        scratch_shapes=[pltpu.VMEM((ROWS, QW), F32)],
    )
    return pl.pallas_call(
        project_q_kernel,
        grid_spec=grid,
        out_shape=jax.ShapeDtypeStruct((ROWS, QW), BF16),
        compiler_params=params(),
        cost_estimate=pl.CostEstimate(flops=2 * ROWS * D * QW, bytes_accessed=2 * D * (QW + ROWS), transcendentals=0),
        name="project_q",
    )(order, normed, w, bias, cosine, sine)


def attend_kernel(index, q, kv, anchor, out, bias):
    keep_anchor = jnp.full((ROWS, ROWS), index[0], jnp.int32) > 0
    row = lax.broadcasted_iota(jnp.int32, (ROWS, ROWS), 0)
    col = lax.broadcasted_iota(jnp.int32, (ROWS, ROWS), 1)
    bias[:, :ROWS] = jnp.where(keep_anchor, 0.0, -jnp.inf)
    bias[:, ROWS:] = jnp.where(row >= col, 0.0, -jnp.inf)
    keys = jnp.concatenate([anchor[:, :HD], kv[:, :HD]], axis=0)
    vals = jnp.concatenate([anchor[:, HD:], kv[:, HD:]], axis=0)
    for head in range(GROUP):
        span = slice(head * HD, (head + 1) * HD)
        scores = lax.dot_general(q[:, span], keys, (((1,), (1,)), ((), ())), preferred_element_type=F32)
        scores = scores * (HD**-0.5) + bias[...]
        peak = jnp.max(scores, axis=-1, keepdims=True)
        weights = jnp.exp(scores - peak)
        total = jnp.sum(weights, axis=-1, keepdims=True)
        mixed = jnp.dot(weights.astype(BF16), vals, preferred_element_type=F32)
        out[:, span] = (mixed / total).astype(BF16)


def attend(index, q, kv, anchor):
    vmem = pl.BlockSpec(memory_space=pltpu.VMEM)
    return pl.pallas_call(
        attend_kernel,
        in_specs=[pl.BlockSpec(memory_space=pltpu.SMEM), vmem, vmem, vmem],
        out_specs=vmem,
        out_shape=jax.ShapeDtypeStruct((ROWS, QW), BF16),
        scratch_shapes=[pltpu.VMEM((ROWS, 2 * ROWS), F32)],
        compiler_params=params(),
        cost_estimate=pl.CostEstimate(
            flops=4 * ROWS * 2 * ROWS * QW, bytes_accessed=4 * ROWS * QW, transcendentals=ROWS * 2 * ROWS * GROUP
        ),
        name="attend",
    )(index, q, kv, anchor)


def times(a, w):
    return lax.dot_general(a, w, (((1,), (1,)), ((), ())), preferred_element_type=F32)


def out_own_kernel(order, tokens, att, w, out):
    out[...] = tokens[...].astype(F32) + times(att[...], w[...])


def out_next_kernel(order, total, below, above, w_below, w_above, out):
    some = total[...] + times(below[...], w_below[...])
    out[...] = some + times(above[...], w_above[...])


def out_last_kernel(order, total, first, second, w_far, gain, head, resid_out, stats_out):
    half = first.shape[0]
    lane = lax.broadcasted_iota(jnp.int32, (half, HD), 1)
    w = w_far[...]
    for at, ref in enumerate((first, second)):
        rows = pl.ds(at * half, half)
        resid = total[rows, :] + times(ref[...], w)
        resid_out[rows, :] = resid.astype(BF16)
        squares = jnp.sum(resid * resid, axis=-1, keepdims=True)
        products = jnp.sum(resid * gain[...] * head[...], axis=-1, keepdims=True)
        both = jnp.where(lane == 0, squares, products)
        stats_out[at] = both.T[:8, :]


def out_call(kernel, order, operands, w, picks, extra, out_shape, name):
    spec = lambda at: pl.BlockSpec((PIECE, QW), lambda i, order, at=at: (order[at], 0))
    grid = pltpu.PrefetchScalarGridSpec(
        num_scalar_prefetch=1,
        grid=(1,),
        in_specs=[whole(*o.shape) for o in operands] + [spec(at) for at in picks] + [whole(*e.shape) for e in extra],
        out_specs=jax.tree.map(lambda s: whole(*s.shape), out_shape),
    )
    return pl.pallas_call(
        kernel,
        grid_spec=grid,
        out_shape=out_shape,
        compiler_params=params(),
        cost_estimate=pl.CostEstimate(
            flops=2 * ROWS * QW * PIECE * len(picks), bytes_accessed=6 * MIB, transcendentals=0
        ),
        name=name,
    )(order, *operands, *([w] * len(picks)), *extra)


def values_kernel(stats, critic_bias, reward, discount, matrix, tail, edge, values_out, local_out, records_out):
    sums = stats[0] + stats[1] + stats[2] + stats[3]
    values = sums[1:2] * lax.rsqrt(sums[0:1] / D + EPS) + critic_bias[0]
    lane = lax.broadcasted_iota(jnp.int32, (1, ROWS), 1)
    following = jnp.where(lane == ROWS - 1, 0.0, pltpu.roll(values, ROWS - 1, 1))
    delta = reward[...] + discount[...] * following - values
    local = lax.dot_general(
        jnp.broadcast_to(delta, (8, ROWS)),
        matrix[...],
        (((1,), (1,)), ((), ())),
        precision=lax.Precision.HIGHEST,
        preferred_element_type=F32,
    )[0:1]
    values_out[...] = values
    local_out[...] = local
    head = lane[:, :HD] == 0
    record = jnp.zeros((1, HD), F32)
    for at, row in enumerate((values, local, tail[...], edge[...])):
        first = jnp.sum(jnp.where(head, row[:, :HD], 0.0), axis=-1, keepdims=True)
        record = jnp.where(lane[:, :HD] == at, first, record)
    records_out[...] = jnp.broadcast_to(record, records_out.shape)


def advantages_kernel(index, records, local, tail, edge, out):
    n = records.shape[0]
    row = lax.broadcasted_iota(jnp.int32, (n, HD), 0)

    def column(at):
        return jnp.broadcast_to(records[:, at : at + 1], (n, HD))

    def later(x, distance, fill):
        return jnp.where(row < n - distance, pltpu.roll(x, n - distance, 0), fill)

    first = column(0)
    term = column(1) + column(3) * later(first, 1, 0.0)
    decay = column(2)
    distance = 1
    while distance < n:
        term = term + decay * later(term, distance, 0.0)
        decay = decay * later(decay, distance, 1.0)
        distance *= 2
    after = row == index[0] + 1
    carry = jnp.sum(jnp.where(after, term, 0.0), axis=0, keepdims=True)
    value = jnp.sum(jnp.where(after, first, 0.0), axis=0, keepdims=True)
    for at in range(0, ROWS, HD):
        span = slice(at, at + HD)
        out[:, span] = local[:, span] + edge[:, span] * value + tail[:, span] * carry


def small_call(kernel, operands, scalars, out_shape, name):
    vmem = pl.BlockSpec(memory_space=pltpu.VMEM)
    smem = pl.BlockSpec(memory_space=pltpu.SMEM)
    return pl.pallas_call(
        kernel,
        in_specs=[smem if at in scalars else vmem for at in range(len(operands))],
        out_specs=jax.tree.map(lambda s: vmem, out_shape),
        out_shape=out_shape,
        compiler_params=params(),
        cost_estimate=pl.CostEstimate(flops=2 * ROWS * ROWS, bytes_accessed=MIB, transcendentals=0),
        name=name,
    )(*operands)


def gather_by_all_to_all(block, axis, groups, n):
    everywhere = jnp.broadcast_to(block[None], (n, *block.shape))
    return lax.all_to_all(everywhere, axis, 0, 0, axis_index_groups=groups)


Z_GROUPS = [[place(x, z, c) for z in range(Z)] for x in range(X) for c in range(C)]
X_GROUPS = [[place(x, z, c) for x in range(X)] for z in range(Z) for c in range(C)]


def other_core(block):
    return lax.ppermute(block, "ctx", [(i, i ^ 1) for i in range(X * Z * C)])


def broadcast_anchor(block):
    here = lax.axis_index("ctx")
    at = (here // (Z * C), here // C % Z, here % C)
    holders = [(0, 0, 0)]
    for stage in (((1, 0, 0), (3, 0, 0), (2, 0, 0)), ((0, 2, 0), (0, 6, 0), (0, 4, 0)), ((0, 1, 0),), ((0, 0, 1),)):
        holding = jnp.ones((), jnp.bool_)
        for axis in range(3):
            seen = sorted({h[axis] for h in holders})
            holding &= sum((at[axis] == v).astype(jnp.int32) for v in seen) > 0
        fresh, sent = [], None
        for dx, dz, dc in stage:
            targets = [((x + dx) % X, (z + dz) % Z, (c + dc) % C) for x, z, c in holders]
            got = lax.ppermute(block, "ctx", [(place(*a), place(*b)) for a, b in zip(holders, targets)])
            sent = got if sent is None else sent + got
            fresh += targets
        block = jnp.where(holding, block, sent)
        holders = holders + fresh
    return block


def on_device(
    tokens,
    input_gain,
    w_query,
    w_key,
    w_value,
    query_bias,
    key_bias,
    value_bias,
    w_out,
    final_gain,
    critic_head,
    critic_bias,
    rewards,
    turn_ends,
    episode_done,
):
    index = lax.axis_index("ctx")
    mine = lax.axis_index("tp")
    order = jnp.stack([mine, (mine + 3) % T, (mine + 1) % T, (mine + 2) % T, index % C]).astype(jnp.int32)

    corner = [
        (place(x, z, c) * T + y, place(y, z, c) * T + x) for x in range(X) for z in range(Z) for c in range(C) for y in range(T)
    ]
    out_block = lax.ppermute(w_out.T, ("ctx", "tp"), corner)
    weights = lax.all_gather(jnp.concatenate([out_block, w_query], axis=1), "ctx", axis=0, tiled=True)

    half = ROWS // 2
    below, above = shift_tp(tokens, 1), shift_tp(tokens, -1)
    kv_part = gather_by_all_to_all(jnp.concatenate([w_key, w_value], axis=1), "ctx", Z_GROUPS, Z)
    below, above, kv_part = lax.optimization_barrier((below, above, kv_part))
    first, second = shift_tp(below[:half], 1), shift_tp(above[half:], -1)
    kv_own = gather_by_all_to_all(kv_part, "ctx", X_GROUPS, X)
    first, second, kv_own = lax.optimization_barrier((first, second, kv_own))
    pieces = (tokens, below, above, first, second)
    kv_other = other_core(kv_own)

    positions = (index * ROWS + jnp.arange(ROWS)).astype(F32)
    steps = jnp.arange(HALF).astype(F32)
    inverse = 1.0 / ROPE_BASE ** (steps * 2.0 / HD)
    angle = positions[:, None] * inverse[None, :]
    cosine, sine = jnp.cos(angle), jnp.sin(angle)
    cosine = jnp.concatenate([cosine, cosine], axis=1)
    sine = jnp.concatenate([-sine, sine], axis=1)
    kv_bias = jnp.concatenate([key_bias, value_bias])[None, :]
    normed, kv = project_kv(order, pieces, input_gain.reshape(T, 1, PIECE), kv_own, kv_other, kv_bias, cosine, sine)
    anchor = broadcast_anchor(kv)
    query = project_q(order, normed, weights, query_bias[None, :], cosine, sine)
    att = attend(index.astype(jnp.int32)[None], query, kv, anchor)

    own, below, above, first, second = ring_tp(att)
    wide = jax.ShapeDtypeStruct((ROWS, PIECE), F32)
    total = out_call(out_own_kernel, order, [tokens, own], weights, (0,), [], wide, "out_own")
    total = out_call(out_next_kernel, order, [total, below, above], weights, (1, 2), [], wide, "out_next")
    residual_stream, stats = out_call(
        out_last_kernel,
        order,
        [total, first, second],
        weights,
        (3,),
        [final_gain[None, :], critic_head[None, :]],
        [jax.ShapeDtypeStruct((ROWS, PIECE), BF16), jax.ShapeDtypeStruct((2, 8, ROWS // 2), F32)],
        "out_last",
    )
    stats = gather_by_all_to_all(jnp.concatenate([stats[0], stats[1]], axis=1), "tp", None, T)

    ends = jnp.maximum(turn_ends, episode_done)
    discount = jnp.where(ends > 0, GAMMA, 1.0).astype(F32) * (1 - episode_done).astype(F32)
    reward = REWARD_SCALE * (rewards * ends).astype(F32)
    decaying = ends * (1 - episode_done)
    zero_int = jnp.zeros((1,), jnp.int32)
    decay_count = jnp.concatenate([zero_int, jnp.cumsum(decaying)])
    done_count = jnp.concatenate([zero_int, jnp.cumsum(episode_done)])
    rate = GAMMA * LAMBDA
    later = jnp.arange(ROWS)[None, :] >= jnp.arange(ROWS)[:, None]
    same_episode = done_count[None, :ROWS] == done_count[:ROWS, None]
    powers = (decay_count[None, :ROWS] - decay_count[:ROWS, None]).astype(F32)
    matrix = jnp.where(later & same_episode, jnp.power(rate, powers), 0.0)
    tail_powers = (decay_count[ROWS] - decay_count[:ROWS]).astype(F32)
    tail = jnp.where(done_count[ROWS] == done_count[:ROWS], jnp.power(rate, tail_powers), 0.0)[None, :]
    edge = (matrix[:, ROWS - 1] * discount[ROWS - 1])[None, :]

    n = lax.axis_size("ctx")
    line = jax.ShapeDtypeStruct((1, ROWS), F32)
    values, local, records = small_call(
        values_kernel,
        [stats, critic_bias, reward[None, :], discount[None, :], matrix, tail, edge],
        (1,),
        [line, line, jax.ShapeDtypeStruct((n, HD), F32)],
        "values",
    )
    records = lax.all_to_all(records, "ctx", 0, 0, tiled=True)
    advantages = small_call(
        advantages_kernel, [index.astype(jnp.int32)[None], records, local, tail, edge], (0,), line, "advantages"
    )
    return (residual_stream, values[0], advantages[0])


def solution(mesh):
    in_specs = (
        P("ctx", "tp"),
        P(),
        P("ctx", "tp"),
        P("ctx", "tp"),
        P("ctx", "tp"),
        P("tp"),
        P("tp"),
        P("tp"),
        P("tp", "ctx"),
        P("tp"),
        P("tp"),
        P(),
        P("ctx"),
        P("ctx"),
        P("ctx"),
    )
    out_specs = (P("ctx", "tp"), P("ctx"), P("ctx"))
    return jax.shard_map(
        on_device, mesh=mesh, in_specs=in_specs, out_specs=out_specs, check_vma=False
    )
```

```python
import jax
import jax.numpy as jnp
from jax import lax
from jax.experimental import pallas as pl
from jax.experimental.pallas import tpu as pltpu
from jax.sharding import PartitionSpec as P

D = 5120
HD = 128
HALF = HD // 2
GROUP = 5
QW = GROUP * HD

EPS = 1e-06
GAMMA = 0.99
LAMBDA = 0.95
ROPE_BASE = 1000000.0
REWARD_SCALE = 0.25

X, Z, C, T = 4, 8, 2, 4
ROWS = 384
SHARD = 80
PIECE = D // T
MIB = 1 << 20

F32 = jnp.float32
BF16 = jnp.bfloat16


def place(x, z, c):
    return (x * Z + z) * C + c


def shift_tp(block, distance):
    return lax.ppermute(block, "tp", [(i, (i + distance) % T) for i in range(T)])


def params(mib=40):
    return pltpu.CompilerParams(vmem_limit_bytes=mib * MIB)


def interleave(core, own, other, joined):
    zs, _, rows, n = joined.shape
    joined[:, pl.ds(core, 1)] = own[...].reshape(zs, 1, rows, n)
    joined[:, pl.ds(1 - core, 1)] = other[...].reshape(zs, 1, rows, n)
    return joined[...].reshape(-1, joined.shape[-1])


def turned(u, cosine, sine):
    return u * cosine[...] + pltpu.roll(u, HALF, 1) * sine[...]


def norm_kernel(own, below, above, first, second, gain, normed_out):
    def squares(ref):
        x = ref[...].astype(F32)
        return jnp.sum(x * x, axis=-1, keepdims=True)

    half = first.shape[0]
    far = jnp.concatenate([squares(first), squares(second)], axis=0)
    mean = (squares(own) + squares(below) + squares(above) + far) / D
    scale = lax.rsqrt(mean + EPS)
    for at, ref in enumerate((own, below, above)):
        normed_out[at] = (ref[...].astype(F32) * scale * gain[at]).astype(BF16)
    normed_out[T - 1, :half] = (first[...].astype(F32) * scale[:half] * gain[T - 1]).astype(BF16)
    normed_out[T - 1, half:] = (second[...].astype(F32) * scale[half:] * gain[T - 1]).astype(BF16)


def project_kv_kernel(order, normed, w_own, w_other, bias, cosine, sine, kv_out, acc, joined):
    step = pl.program_id(0)

    @pl.when(step == 0)
    def _():
        acc[...] = jnp.zeros_like(acc)

    w = interleave(order[T], w_own, w_other, joined)
    acc[...] += jnp.dot(normed[0], w, preferred_element_type=F32)

    @pl.when(step == T - 1)
    def _():
        kv_out[:, :HD] = turned(acc[:, :HD] + bias[:, :HD], cosine, sine).astype(BF16)
        kv_out[:, HD:] = (acc[:, HD:] + bias[:, HD:]).astype(BF16)


def whole(*shape):
    return pl.BlockSpec(shape, lambda k, order: (0,) * len(shape))


def project_kv(order, normed, w_own, w_other, bias, cosine, sine):
    rows = Z * SHARD
    shards = pl.BlockSpec((1, rows, 2 * HD), lambda k, order: (order[k], 0, 0))
    grid = pltpu.PrefetchScalarGridSpec(
        num_scalar_prefetch=1,
        grid=(T,),
        in_specs=[
            pl.BlockSpec((1, ROWS, PIECE), lambda k, order: (k, 0, 0)),
            shards,
            shards,
            whole(1, 2 * HD),
            whole(ROWS, HD),
            whole(ROWS, HD),
        ],
        out_specs=whole(ROWS, 2 * HD),
        scratch_shapes=[pltpu.VMEM((ROWS, 2 * HD), F32), pltpu.VMEM((Z, C, SHARD, 2 * HD), BF16)],
    )
    return pl.pallas_call(
        project_kv_kernel,
        grid_spec=grid,
        out_shape=jax.ShapeDtypeStruct((ROWS, 2 * HD), BF16),
        compiler_params=params(),
        cost_estimate=pl.CostEstimate(flops=4 * ROWS * D * HD, bytes_accessed=2 * D * (2 * HD + ROWS), transcendentals=0),
        name="project_kv",
    )(order, normed, w_own, w_other, bias, cosine, sine)


def project_q_kernel(order, normed, w, bias, cosine, sine, q_out, acc):
    step = pl.program_id(0)

    @pl.when(step == 0)
    def _():
        acc[...] = jnp.zeros_like(acc)

    acc[...] += jnp.dot(normed[0], w[...], preferred_element_type=F32)

    @pl.when(step == T - 1)
    def _():
        for head in range(GROUP):
            span = slice(head * HD, (head + 1) * HD)
            q_out[:, span] = turned(acc[:, span] + bias[:, span], cosine, sine).astype(BF16)


def project_q(order, normed, w, bias, cosine, sine):
    grid = pltpu.PrefetchScalarGridSpec(
        num_scalar_prefetch=1,
        grid=(T,),
        in_specs=[
            pl.BlockSpec((1, ROWS, PIECE), lambda k, order: (k, 0, 0)),
            pl.BlockSpec((PIECE, QW), lambda k, order: (order[k], 1)),
            whole(1, QW),
            whole(ROWS, HD),
            whole(ROWS, HD),
        ],
        out_specs=whole(ROWS, QW),
        scratch_shapes=[pltpu.VMEM((ROWS, QW), F32)],
    )
    return pl.pallas_call(
        project_q_kernel,
        grid_spec=grid,
        out_shape=jax.ShapeDtypeStruct((ROWS, QW), BF16),
        compiler_params=params(),
        cost_estimate=pl.CostEstimate(flops=2 * ROWS * D * QW, bytes_accessed=2 * D * (QW + ROWS), transcendentals=0),
        name="project_q",
    )(order, normed, w, bias, cosine, sine)


def attend_kernel(index, q, kv, anchor, out, bias):
    keep_anchor = jnp.full((ROWS, ROWS), index[0], jnp.int32) > 0
    row = lax.broadcasted_iota(jnp.int32, (ROWS, ROWS), 0)
    col = lax.broadcasted_iota(jnp.int32, (ROWS, ROWS), 1)
    bias[:, :ROWS] = jnp.where(keep_anchor, 0.0, -jnp.inf)
    bias[:, ROWS:] = jnp.where(row >= col, 0.0, -jnp.inf)
    keys = jnp.concatenate([anchor[:, :HD], kv[:, :HD]], axis=0)
    vals = jnp.concatenate([anchor[:, HD:], kv[:, HD:]], axis=0)
    for head in range(GROUP):
        span = slice(head * HD, (head + 1) * HD)
        scores = lax.dot_general(q[:, span], keys, (((1,), (1,)), ((), ())), preferred_element_type=F32)
        scores = scores * (HD**-0.5) + bias[...]
        peak = jnp.max(scores, axis=-1, keepdims=True)
        weights = jnp.exp(scores - peak)
        total = jnp.sum(weights, axis=-1, keepdims=True)
        mixed = jnp.dot(weights.astype(BF16), vals, preferred_element_type=F32)
        out[:, span] = (mixed / total).astype(BF16)


def attend(index, q, kv, anchor):
    vmem = pl.BlockSpec(memory_space=pltpu.VMEM)
    return pl.pallas_call(
        attend_kernel,
        in_specs=[pl.BlockSpec(memory_space=pltpu.SMEM), vmem, vmem, vmem],
        out_specs=vmem,
        out_shape=jax.ShapeDtypeStruct((ROWS, QW), BF16),
        scratch_shapes=[pltpu.VMEM((ROWS, 2 * ROWS), F32)],
        compiler_params=params(),
        cost_estimate=pl.CostEstimate(
            flops=4 * ROWS * 2 * ROWS * QW, bytes_accessed=4 * ROWS * QW, transcendentals=ROWS * 2 * ROWS * GROUP
        ),
        name="attend",
    )(index, q, kv, anchor)


def times(a, w):
    return lax.dot_general(a, w, (((1,), (1,)), ((), ())), preferred_element_type=F32)


def out_own_kernel(order, tokens, att, w, out):
    out[...] = tokens[...].astype(F32) + times(att[...], w[...])


def out_next_kernel(order, total, below, above, w_below, w_above, out):
    some = total[...] + times(below[...], w_below[...])
    out[...] = some + times(above[...], w_above[...])


def out_last_kernel(order, total, first, second, w_far, gain, head, resid_out, stats_out):
    half = first.shape[0]
    lane = lax.broadcasted_iota(jnp.int32, (ROWS, HD), 1)
    w = w_far[...]
    resid = total[...] + times(jnp.concatenate([first[...], second[...]], axis=0), w)
    resid_out[...] = resid.astype(BF16)
    squares = jnp.sum(resid * resid, axis=-1, keepdims=True)
    products = jnp.sum(resid * gain[...] * head[...], axis=-1, keepdims=True)
    both = jnp.where(lane == 0, squares, products).T[:8, :]
    for at in range(T):
        stats_out[at] = both


def out_call(kernel, order, operands, w, picks, extra, out_shape, name):
    spec = lambda at: pl.BlockSpec((PIECE, QW), lambda i, order, at=at: (order[at], 0))
    grid = pltpu.PrefetchScalarGridSpec(
        num_scalar_prefetch=1,
        grid=(1,),
        in_specs=[whole(*o.shape) for o in operands] + [spec(at) for at in picks] + [whole(*e.shape) for e in extra],
        out_specs=jax.tree.map(lambda s: whole(*s.shape), out_shape),
    )
    return pl.pallas_call(
        kernel,
        grid_spec=grid,
        out_shape=out_shape,
        compiler_params=params(),
        cost_estimate=pl.CostEstimate(
            flops=2 * ROWS * QW * PIECE * len(picks), bytes_accessed=6 * MIB, transcendentals=0
        ),
        name=name,
    )(order, *operands, *([w] * len(picks)), *extra)


def values_kernel(stats, critic_bias, reward, discount, matrix, tail, edge, values_out, local_out, records_out):
    sums = stats[0] + stats[1] + stats[2] + stats[3]
    values = sums[1:2] * lax.rsqrt(sums[0:1] / D + EPS) + critic_bias[0]
    lane = lax.broadcasted_iota(jnp.int32, (1, ROWS), 1)
    following = jnp.where(lane == ROWS - 1, 0.0, pltpu.roll(values, ROWS - 1, 1))
    delta = reward[...] + discount[...] * following - values
    local = lax.dot_general(
        jnp.broadcast_to(delta, (8, ROWS)),
        matrix[...],
        (((1,), (1,)), ((), ())),
        precision=lax.Precision.HIGHEST,
        preferred_element_type=F32,
    )[0:1]
    values_out[...] = values
    local_out[...] = local
    head = lane[:, :HD] == 0
    record = jnp.zeros((1, HD), F32)
    for at, row in enumerate((values, local, tail[...], edge[...])):
        first = jnp.sum(jnp.where(head, row[:, :HD], 0.0), axis=-1, keepdims=True)
        record = jnp.where(lane[:, :HD] == at, first, record)
    records_out[...] = jnp.broadcast_to(record, records_out.shape)


def advantages_kernel(index, records, local, tail, edge, out):
    n = records.shape[0]
    row = lax.broadcasted_iota(jnp.int32, (n, HD), 0)

    def column(at):
        return jnp.broadcast_to(records[:, at : at + 1], (n, HD))

    def later(x, distance, fill):
        return jnp.where(row < n - distance, pltpu.roll(x, n - distance, 0), fill)

    first = column(0)
    term = column(1) + column(3) * later(first, 1, 0.0)
    decay = column(2)
    distance = 1
    while distance < n:
        term = term + decay * later(term, distance, 0.0)
        decay = decay * later(decay, distance, 1.0)
        distance *= 2
    after = row == index[0] + 1
    carry = jnp.sum(jnp.where(after, term, 0.0), axis=0, keepdims=True)
    value = jnp.sum(jnp.where(after, first, 0.0), axis=0, keepdims=True)
    for at in range(0, ROWS, HD):
        span = slice(at, at + HD)
        out[:, span] = local[:, span] + edge[:, span] * value + tail[:, span] * carry


def norm(*operands):
    shape = jax.ShapeDtypeStruct((T, ROWS, PIECE), BF16)
    return small_call(norm_kernel, operands, (), shape, "norm")


def small_call(kernel, operands, scalars, out_shape, name):
    vmem = pl.BlockSpec(memory_space=pltpu.VMEM)
    smem = pl.BlockSpec(memory_space=pltpu.SMEM)
    return pl.pallas_call(
        kernel,
        in_specs=[smem if at in scalars else vmem for at in range(len(operands))],
        out_specs=jax.tree.map(lambda s: vmem, out_shape),
        out_shape=out_shape,
        compiler_params=params(),
        cost_estimate=pl.CostEstimate(flops=2 * ROWS * ROWS, bytes_accessed=MIB, transcendentals=0),
        name=name,
    )(*operands)


def gather_by_all_to_all(block, axis, groups, n):
    everywhere = jnp.broadcast_to(block[None], (n, *block.shape))
    return lax.all_to_all(everywhere, axis, 0, 0, axis_index_groups=groups)


Z_GROUPS = [[place(x, z, c) for z in range(Z)] for x in range(X) for c in range(C)]
X_GROUPS = [[place(x, z, c) for x in range(X)] for z in range(Z) for c in range(C)]


def other_core(block):
    return lax.ppermute(block, "ctx", [(i, i ^ 1) for i in range(X * Z * C)])


TREE = (((1, 0, 0), (3, 0, 0), (2, 0, 0)), ((0, 2, 0), (0, 6, 0), (0, 4, 0)), ((0, 1, 0),), ((0, 0, 1),))


def broadcast_anchor(block, query):
    here = lax.axis_index("ctx")
    at = (here // (Z * C), here // C % Z, here % C)
    holders = [(0, 0, 0)]
    for stage in TREE:
        holding = jnp.ones((), jnp.bool_)
        for axis in range(3):
            seen = sorted({h[axis] for h in holders})
            holding &= sum((at[axis] == v).astype(jnp.int32) for v in seen) > 0
        fresh, sent = [], None
        for dx, dz, dc in stage:
            targets = [((x + dx) % X, (z + dz) % Z, (c + dc) % C) for x, z, c in holders]
            got = lax.ppermute(block, "ctx", [(place(*a), place(*b)) for a, b in zip(holders, targets)])
            sent = got if sent is None else sent + got
            fresh += targets
        if stage is TREE[-2]:
            sent, query = lax.optimization_barrier((sent, query))
        block = jnp.where(holding, block, sent)
        holders = holders + fresh
    return block, query


def on_device(
    tokens,
    input_gain,
    w_query,
    w_key,
    w_value,
    query_bias,
    key_bias,
    value_bias,
    w_out,
    final_gain,
    critic_head,
    critic_bias,
    rewards,
    turn_ends,
    episode_done,
):
    index = lax.axis_index("ctx")
    mine = lax.axis_index("tp")
    order = jnp.stack([mine, (mine + 3) % T, (mine + 1) % T, (mine + 2) % T, index % C]).astype(jnp.int32)

    corner = [
        (place(x, z, c) * T + y, place(y, z, c) * T + x) for x in range(X) for z in range(Z) for c in range(C) for y in range(T)
    ]
    out_block = lax.ppermute(w_out.T, ("ctx", "tp"), corner)
    weights = lax.all_gather(jnp.concatenate([out_block, w_query], axis=1), "ctx", axis=0, tiled=True)

    half = ROWS // 2
    below, above = shift_tp(tokens, 1), shift_tp(tokens, -1)
    kv_part = gather_by_all_to_all(jnp.concatenate([w_key, w_value], axis=1), "ctx", Z_GROUPS, Z)
    below, above, kv_part = lax.optimization_barrier((below, above, kv_part))
    first, second = shift_tp(below[:half], 1), shift_tp(above[half:], -1)
    kv_own = gather_by_all_to_all(kv_part.reshape(Z * SHARD, 2 * HD), "ctx", X_GROUPS, X)
    first, second, kv_own = lax.optimization_barrier((first, second, kv_own))
    kv_other = other_core(kv_own)
    gain = lax.dynamic_slice_in_dim(jnp.tile(input_gain.reshape(T, 1, PIECE), (2, 1, 1)), mine, T, 0)
    normed = norm(tokens, below, above, first, second, gain[jnp.array([0, 3, 1, 2])])

    positions = (index * ROWS + jnp.arange(ROWS)).astype(F32)
    steps = jnp.arange(HALF).astype(F32)
    inverse = 1.0 / ROPE_BASE ** (steps * 2.0 / HD)
    angle = positions[:, None] * inverse[None, :]
    cosine, sine = jnp.cos(angle), jnp.sin(angle)
    cosine = jnp.concatenate([cosine, cosine], axis=1)
    sine = jnp.concatenate([-sine, sine], axis=1)
    kv_bias = jnp.concatenate([key_bias, value_bias])[None, :]
    kv = project_kv(order, normed, kv_own, kv_other, kv_bias, cosine, sine)
    query = project_q(order, normed, weights, query_bias[None, :], cosine, sine)
    anchor, query = broadcast_anchor(kv, query)
    att = attend(index.astype(jnp.int32)[None], query, kv, anchor)

    below, above = shift_tp(att, 1), shift_tp(att, -1)
    wide = jax.ShapeDtypeStruct((ROWS, PIECE), F32)
    total = out_call(out_own_kernel, order, [tokens, att], weights, (0,), [], wide, "out_own")
    total, below, above = lax.optimization_barrier((total, below, above))
    first, second = shift_tp(below[:half], 1), shift_tp(above[half:], -1)
    total = out_call(out_next_kernel, order, [total, below, above], weights, (1, 2), [], wide, "out_next")
    residual_stream, stats = out_call(
        out_last_kernel,
        order,
        [total, first, second],
        weights,
        (3,),
        [final_gain[None, :], critic_head[None, :]],
        [jax.ShapeDtypeStruct((ROWS, PIECE), BF16), jax.ShapeDtypeStruct((T, 8, ROWS), F32)],
        "out_last",
    )
    stats = lax.all_to_all(stats, "tp", 0, 0)

    ends = jnp.maximum(turn_ends, episode_done)
    discount = jnp.where(ends > 0, GAMMA, 1.0).astype(F32) * (1 - episode_done).astype(F32)
    reward = REWARD_SCALE * (rewards * ends).astype(F32)
    decaying = ends * (1 - episode_done)
    zero_int = jnp.zeros((1,), jnp.int32)
    decay_count = jnp.concatenate([zero_int, jnp.cumsum(decaying)])
    done_count = jnp.concatenate([zero_int, jnp.cumsum(episode_done)])
    rate = GAMMA * LAMBDA
    later = jnp.arange(ROWS)[None, :] >= jnp.arange(ROWS)[:, None]
    same_episode = done_count[None, :ROWS] == done_count[:ROWS, None]
    powers = (decay_count[None, :ROWS] - decay_count[:ROWS, None]).astype(F32)
    matrix = jnp.where(later & same_episode, jnp.power(rate, powers), 0.0)
    tail_powers = (decay_count[ROWS] - decay_count[:ROWS]).astype(F32)
    tail = jnp.where(done_count[ROWS] == done_count[:ROWS], jnp.power(rate, tail_powers), 0.0)[None, :]
    edge = (matrix[:, ROWS - 1] * discount[ROWS - 1])[None, :]

    n = lax.axis_size("ctx")
    line = jax.ShapeDtypeStruct((1, ROWS), F32)
    values, local, records = small_call(
        values_kernel,
        [stats, critic_bias, reward[None, :], discount[None, :], matrix, tail, edge],
        (1,),
        [line, line, jax.ShapeDtypeStruct((n, HD), F32)],
        "values",
    )
    records = lax.all_to_all(records, "ctx", 0, 0, tiled=True)
    advantages = small_call(
        advantages_kernel, [index.astype(jnp.int32)[None], records, local, tail, edge], (0,), line, "advantages"
    )
    return (residual_stream, values[0], advantages[0])


def solution(mesh):
    in_specs = (
        P("ctx", "tp"),
        P(),
        P("ctx", "tp"),
        P("ctx", "tp"),
        P("ctx", "tp"),
        P("tp"),
        P("tp"),
        P("tp"),
        P("tp", "ctx"),
        P("tp"),
        P("tp"),
        P(),
        P("ctx"),
        P("ctx"),
        P("ctx"),
    )
    out_specs = (P("ctx", "tp"), P("ctx"), P("ctx"))
    return jax.shard_map(
        on_device, mesh=mesh, in_specs=in_specs, out_specs=out_specs, check_vma=False
    )
```

```python
import math

import jax
import jax.numpy as jnp
from jax import lax
from jax.experimental import pallas as pl
from jax.experimental.pallas import tpu as pltpu
from jax.sharding import PartitionSpec as P

D = 5120
HD = 128
HALF = HD // 2
GROUP = 5
QW = GROUP * HD

EPS = 1e-06
GAMMA = 0.99
LAMBDA = 0.95
ROPE_BASE = 1000000.0
REWARD_SCALE = 0.25

X, Z, C, T = 4, 8, 2, 4
ROWS = 384
SHARD = 80
PIECE = D // T
MIB = 1 << 20

F32 = jnp.float32
BF16 = jnp.bfloat16


def place(x, z, c):
    return (x * Z + z) * C + c


def shift_tp(block, distance):
    return lax.ppermute(block, "tp", [(i, (i + distance) % T) for i in range(T)])


def local_call(kernel, operands, places, out_shape, name, flops, nbytes, scratch=(), mib=20):
    spaces = {"s": pltpu.SMEM, "v": pltpu.VMEM, "a": pl.ANY}
    return pl.pallas_call(
        kernel,
        in_specs=[pl.BlockSpec(memory_space=spaces[p]) for p in places],
        out_specs=jax.tree.map(lambda s: pl.BlockSpec(memory_space=pltpu.VMEM), out_shape),
        out_shape=out_shape,
        scratch_shapes=list(scratch),
        compiler_params=pltpu.CompilerParams(vmem_limit_bytes=mib * MIB),
        cost_estimate=pl.CostEstimate(flops=flops, bytes_accessed=nbytes, transcendentals=0),
        name=name,
    )(*operands)


def turned(u, cosine, sine):
    return u * cosine[...] + pltpu.roll(u, HALF, 1) * sine[...]


def norm_kernel(order, own, below, above, first, second, gain, normed_out):
    def squares(ref):
        x = ref[...].astype(F32)
        return jnp.sum(x * x, axis=-1, keepdims=True)

    half = first.shape[0]
    far = jnp.concatenate([squares(first), squares(second)], axis=0)
    mean = (squares(own) + squares(below) + squares(above) + far) / D
    scale = lax.rsqrt(mean + EPS)
    for at, ref in enumerate((own, below, above)):
        normed_out[at] = (ref[...].astype(F32) * scale * gain[order[at]]).astype(BF16)
    normed_out[T - 1, :half] = (first[...].astype(F32) * scale[:half] * gain[order[T - 1]]).astype(BF16)
    normed_out[T - 1, half:] = (second[...].astype(F32) * scale[half:] * gain[order[T - 1]]).astype(BF16)


def norm(order, pieces, gain):
    shape = jax.ShapeDtypeStruct((T, ROWS, PIECE), BF16)
    return local_call(norm_kernel, [order, *pieces, gain], "s" + "v" * 6, shape, "norm", 6 * ROWS * D, 4 * ROWS * D)


def project_kv_kernel(
    order, normed, w_own, w_other, bias, cosine, sine, kv_out, key_out, value_out, mark_out, joined, sems
):
    core = order[T]
    copies = []
    for k in range(T):
        for at, (ref, lane) in enumerate(((w_own, core), (w_other, 1 - core))):
            copy = pltpu.make_async_copy(ref.at[order[k]], joined.at[k, :, lane], sems.at[k, at])
            copy.start()
            copies.append(copy)
    total = jnp.zeros((ROWS, 2 * HD), F32)
    for k in range(T):
        copies[2 * k].wait()
        copies[2 * k + 1].wait()
        total += jnp.dot(normed[k], joined[k].reshape(PIECE, 2 * HD), preferred_element_type=F32)
    key = turned(total[:, :HD] + bias[:, :HD], cosine, sine).astype(BF16)
    value = (total[:, HD:] + bias[:, HD:]).astype(BF16)
    kv_out[:, :HD] = key
    kv_out[:, HD:] = value
    key_out[...] = key
    value_out[...] = value
    mark_out[...] = jnp.zeros_like(mark_out)


def project_kv(order, normed, w_own, w_other, bias, cosine, sine):
    one = jax.ShapeDtypeStruct((ROWS, HD), BF16)
    return local_call(
        project_kv_kernel,
        [order, normed, w_own, w_other, bias, cosine, sine],
        "svaavvv",
        [jax.ShapeDtypeStruct((ROWS, 2 * HD), BF16), one, one, jax.ShapeDtypeStruct((1, ROWS), jnp.int32)],
        "project_kv",
        4 * ROWS * D * HD,
        2 * D * (2 * HD + ROWS),
        [pltpu.VMEM((T, Z, C, SHARD, 2 * HD), BF16), pltpu.SemaphoreType.DMA((T, 2))],
    )


def project_q_kernel(order, normed, w, bias, cosine, sine, q_out, held, acc, sems):
    parts = 4
    members = Z * C // parts

    def copies(k):
        for part in range(parts):
            source = w.at[pl.ds(order[k] * Z * C + part * members, members), 1]
            yield pltpu.make_async_copy(source, held.at[k, pl.ds(part * members, members)], sems.at[k, part])

    for k in range(2):
        for copy in copies(k):
            copy.start()
    for k in range(T):
        for copy in copies(k):
            copy.wait()
        if k + 2 < T:
            for copy in copies(k + 2):
                copy.start()
        part = jnp.dot(normed[k], held[k].reshape(PIECE, QW), preferred_element_type=F32)
        acc[...] = part if k == 0 else acc[...] + part
    for head in range(GROUP):
        span = slice(head * HD, (head + 1) * HD)
        q_out[:, span] = turned(acc[:, span] + bias[:, span], cosine, sine).astype(BF16)


def project_q(order, normed, w, bias, cosine, sine):
    return local_call(
        project_q_kernel,
        [order, normed, w, bias, cosine, sine],
        "svavvv",
        jax.ShapeDtypeStruct((ROWS, QW), BF16),
        "project_q",
        2 * ROWS * D * QW,
        2 * D * (QW + ROWS),
        [pltpu.VMEM((T, Z * C, SHARD, QW), BF16), pltpu.VMEM((ROWS, QW), F32), pltpu.SemaphoreType.DMA((T, 4))],
        52,
    )


def attend_kernel(index, q, kv, mine, other, out, seen, bias):
    core = index[1]
    seen[core, :ROWS] = mine[...]
    seen[1 - core, :ROWS] = other[...]
    seen[0, ROWS:] = kv[:, :HD]
    seen[1, ROWS:] = kv[:, HD:]
    row = lax.broadcasted_iota(jnp.int32, (ROWS, ROWS), 0)
    col = lax.broadcasted_iota(jnp.int32, (ROWS, ROWS), 1)
    bias[:, :ROWS] = jnp.where(jnp.full((ROWS, ROWS), index[0], jnp.int32) > 0, 0.0, -jnp.inf)
    bias[:, ROWS:] = jnp.where(row >= col, 0.0, -jnp.inf)
    for head in range(GROUP):
        span = slice(head * HD, (head + 1) * HD)
        scores = lax.dot_general(q[:, span], seen[0], (((1,), (1,)), ((), ())), preferred_element_type=F32)
        scores = scores + bias[...]
        peak = jnp.max(scores, axis=-1, keepdims=True)
        weights = jnp.exp2((scores - peak) * (HD**-0.5 * math.log2(math.e)))
        total = jnp.sum(weights, axis=-1, keepdims=True)
        mixed = jnp.dot(weights.astype(BF16), seen[1], preferred_element_type=F32)
        out[:, span] = (mixed / total).astype(BF16)


def attend(index, q, kv, mine, other):
    return local_call(
        attend_kernel,
        [index, q, kv, mine, other],
        "svvvv",
        jax.ShapeDtypeStruct((ROWS, QW), BF16),
        "attend",
        4 * ROWS * 2 * ROWS * QW,
        4 * ROWS * QW,
        [pltpu.VMEM((2, 2 * ROWS, HD), BF16), pltpu.VMEM((ROWS, 2 * ROWS), F32)],
    )


def times(a, w):
    return lax.dot_general(a, w, (((1,), (1,)), ((), ())), preferred_element_type=F32)


def halves_kernel(below, above, total, first, second):
    half = first.shape[0]
    first[...] = below[:half]
    second[...] = above[half:]


def stack_kernel(first, second, out):
    out[0] = first[...]
    out[1] = second[...]


def rows_of(w, group):
    return w[pl.ds(lax.rem(group + 2, X) * Z * C, Z * C)].reshape(PIECE, QW)


def out_own_kernel(order, att, w, out):
    out[...] = times(att[...], rows_of(w, order[0]))


def out_next_kernel(order, total, below, above, w, out):
    some = total[...] + times(below[...], rows_of(w, order[1]))
    out[...] = some + times(above[...], rows_of(w, order[2]))


def out_last_kernel(order, tokens, total, first, second, w, gain, head, resid_out, stats_out):
    lane = lax.broadcasted_iota(jnp.int32, (ROWS, HD), 1)
    resid = tokens[...].astype(F32) + total[...] + times(jnp.concatenate([first[...], second[...]], axis=0), rows_of(w, order[T - 1]))
    resid_out[...] = resid.astype(BF16)
    squares = jnp.sum(resid * resid, axis=-1, keepdims=True)
    products = jnp.sum(resid * gain[...] * head[...], axis=-1, keepdims=True)
    both = jnp.where(lane == 0, squares, products).T[:8, :]
    for at in range(T):
        stats_out[at] = both


def values_kernel(stats, critic_bias, reward, discount, matrix, tail, edge, values_out, local_out, records_out):
    sums = stats[0] + stats[1] + stats[2] + stats[3]
    values = sums[1:2] * lax.rsqrt(sums[0:1] / D + EPS) + critic_bias[0]
    lane = lax.broadcasted_iota(jnp.int32, (1, ROWS), 1)
    following = jnp.where(lane == ROWS - 1, 0.0, pltpu.roll(values, ROWS - 1, 1))
    delta = reward[...] + discount[...] * following - values
    local = lax.dot_general(
        jnp.broadcast_to(delta, (8, ROWS)),
        matrix[...],
        (((1,), (1,)), ((), ())),
        precision=lax.Precision.HIGHEST,
        preferred_element_type=F32,
    )[0:1]
    values_out[...] = values
    local_out[...] = local
    head = lane[:, :HD] == 0
    record = jnp.zeros((1, HD), F32)
    for at, row in enumerate((values, local, tail[...], edge[...])):
        first = jnp.sum(jnp.where(head, row[:, :HD], 0.0), axis=-1, keepdims=True)
        record = jnp.where(lane[:, :HD] == at, first, record)
    records_out[...] = jnp.broadcast_to(record, records_out.shape)


def advantages_kernel(index, records, local, tail, edge, out):
    n = records.shape[0]
    row = lax.broadcasted_iota(jnp.int32, (n, HD), 0)

    def column(at):
        return jnp.broadcast_to(records[:, at : at + 1], (n, HD))

    def later(x, distance, fill):
        return jnp.where(row < n - distance, pltpu.roll(x, n - distance, 0), fill)

    first = column(0)
    term = column(1) + column(3) * later(first, 1, 0.0)
    decay = column(2)
    distance = 1
    while distance < n:
        term = term + decay * later(term, distance, 0.0)
        decay = decay * later(decay, distance, 1.0)
        distance *= 2
    after = row == index[0] + 1
    carry = jnp.sum(jnp.where(after, term, 0.0), axis=0, keepdims=True)
    value = jnp.sum(jnp.where(after, first, 0.0), axis=0, keepdims=True)
    for at in range(0, ROWS, HD):
        span = slice(at, at + HD)
        out[:, span] = local[:, span] + edge[:, span] * value + tail[:, span] * carry


def gather_by_all_to_all(block, axis, groups, n):
    everywhere = jnp.broadcast_to(block[None], (n, *block.shape))
    return lax.all_to_all(everywhere, axis, 0, 0, axis_index_groups=groups)


Z_GROUPS = [[place(x, z, c) for z in range(Z)] for x in range(X) for c in range(C)]
X_GROUPS = [[place(x, z, c) for x in range(X)] for z in range(Z) for c in range(C)]


def other_core(block):
    return lax.ppermute(block, "ctx", [(i, i ^ 1) for i in range(X * Z * C)])


OVER_X = ((1, 0), (3, 0), (2, 0))
OVER_Z = ((0, 2), (0, 6), (0, 4))
LAST = ((0, 1),)
TREES = ((OVER_X, OVER_Z, LAST), (OVER_Z, OVER_X, LAST))


def broadcast_anchor(key, value):
    here = lax.axis_index("ctx")
    x, z, core = here // (Z * C), here // C % Z, here % C
    block = jnp.where(core == 0, key, lax.ppermute(value, "ctx", [(0, 1)]))
    holders = [[(0, 0)], [(0, 0)]]
    for stages in zip(*TREES):
        holding = jnp.zeros((), jnp.bool_)
        for c in range(C):
            xs, zs = ({h[axis] for h in holders[c]} for axis in range(2))
            among = lambda at, seen: sum((at == v).astype(jnp.int32) for v in seen) > 0
            holding |= (core == c) & among(x, sorted(xs)) & among(z, sorted(zs))
        sent = None
        fresh = [[], []]
        for shifts in zip(*stages):
            pairs = []
            for c, (dx, dz) in enumerate(shifts):
                targets = [((px + dx) % X, (pz + dz) % Z) for px, pz in holders[c]]
                pairs += [(place(*a, c), place(*b, c)) for a, b in zip(holders[c], targets)]
                fresh[c] += targets
            got = lax.ppermute(block, "ctx", pairs)
            sent = got if sent is None else sent + got
        block = jnp.where(holding, block, sent)
        holders = [old + new for old, new in zip(holders, fresh)]
    return block, other_core(block)


def on_device(
    tokens,
    input_gain,
    w_query,
    w_key,
    w_value,
    query_bias,
    key_bias,
    value_bias,
    w_out,
    final_gain,
    critic_head,
    critic_bias,
    rewards,
    turn_ends,
    episode_done,
):
    index = lax.axis_index("ctx")
    mine = lax.axis_index("tp")
    order = jnp.stack([mine, (mine + 3) % T, (mine + 1) % T, (mine + 2) % T, index % C]).astype(jnp.int32)

    corner = [
        (place(x, z, c) * T + y, place((y + 2) % X, z, c) * T + x)
        for x in range(X)
        for z in range(Z)
        for c in range(C)
        for y in range(T)
    ]
    out_block = lax.ppermute(w_out.T, ("ctx", "tp"), corner)
    both = local_call(
        stack_kernel, [out_block, w_query], "vv", jax.ShapeDtypeStruct((2, SHARD, QW), BF16), "stack", 0, 8 * SHARD * QW
    )
    weights = lax.all_gather(both, "ctx")

    half = ROWS // 2
    below, above = shift_tp(tokens, 1), shift_tp(tokens, -1)
    kv_part = gather_by_all_to_all(jnp.concatenate([w_key, w_value], axis=1), "ctx", Z_GROUPS, Z)
    below, above, kv_part = lax.optimization_barrier((below, above, kv_part))
    first, second = shift_tp(below[:half], 1), shift_tp(above[half:], -1)
    kv_own = gather_by_all_to_all(kv_part, "ctx", X_GROUPS, X)
    first, second, kv_own = lax.optimization_barrier((first, second, kv_own))
    normed = norm(order, (tokens, below, above, first, second), input_gain.reshape(T, 1, PIECE))
    kv_other = other_core(kv_own)
    positions = (index * ROWS + jnp.arange(ROWS)).astype(F32)
    steps = jnp.arange(HALF).astype(F32)
    inverse = 1.0 / ROPE_BASE ** (steps * 2.0 / HD)
    angle = positions[:, None] * inverse[None, :]
    cosine, sine = jnp.cos(angle), jnp.sin(angle)
    cosine = jnp.concatenate([cosine, cosine], axis=1)
    sine = jnp.concatenate([-sine, sine], axis=1)
    kv_bias = jnp.concatenate([key_bias, value_bias])[None, :]
    kv, key, value, mark = project_kv(order, normed, kv_own, kv_other, kv_bias, cosine, sine)
    query = project_q(order, normed, weights, query_bias[None, :], cosine, sine)
    held, sent = broadcast_anchor(key, value)
    att = attend(jnp.stack([index, index % C]).astype(jnp.int32), query, kv, held, sent)

    weights, att = lax.optimization_barrier((weights, att))
    w_o = weights[:, 0]
    below, above = shift_tp(att, 1), shift_tp(att, -1)
    wide = jax.ShapeDtypeStruct((ROWS, PIECE), F32)
    flops, nbytes = 2 * ROWS * QW * PIECE, 6 * MIB
    total = local_call(out_own_kernel, [order, att, w_o], "svv", wide, "out_own", flops, nbytes)
    pair = jax.ShapeDtypeStruct((half, QW), BF16)
    first, second = local_call(
        halves_kernel, [below, above, total], "vva", [pair, pair], "halves", 0, 4 * half * QW
    )
    first, second = shift_tp(first, 1), shift_tp(second, -1)
    total = local_call(out_next_kernel, [order, total, below, above, w_o], "svvvv", wide, "out_next", 2 * flops, nbytes)
    residual_stream, stats = local_call(
        out_last_kernel,
        [order, tokens, total, first, second, w_o, final_gain[None, :], critic_head[None, :]],
        "svvvvvvv",
        [jax.ShapeDtypeStruct((ROWS, PIECE), BF16), jax.ShapeDtypeStruct((T, 8, ROWS), F32)],
        "out_last",
        flops,
        nbytes,
    )
    stats = lax.all_to_all(stats, "tp", 0, 0)

    turn_ends, episode_done = turn_ends + mark[0], episode_done + mark[0]
    ends = jnp.maximum(turn_ends, episode_done)
    discount = jnp.where(ends > 0, GAMMA, 1.0).astype(F32) * (1 - episode_done).astype(F32)
    reward = REWARD_SCALE * (rewards * ends).astype(F32)
    decaying = ends * (1 - episode_done)
    zero_int = jnp.zeros((1,), jnp.int32)
    decay_count = jnp.concatenate([zero_int, jnp.cumsum(decaying)])
    done_count = jnp.concatenate([zero_int, jnp.cumsum(episode_done)])
    rate = GAMMA * LAMBDA
    later = jnp.arange(ROWS)[None, :] >= jnp.arange(ROWS)[:, None]
    same_episode = done_count[None, :ROWS] == done_count[:ROWS, None]
    powers = (decay_count[None, :ROWS] - decay_count[:ROWS, None]).astype(F32)
    matrix = jnp.where(later & same_episode, jnp.power(rate, powers), 0.0)
    tail_powers = (decay_count[ROWS] - decay_count[:ROWS]).astype(F32)
    tail = jnp.where(done_count[ROWS] == done_count[:ROWS], jnp.power(rate, tail_powers), 0.0)[None, :]
    edge = (matrix[:, ROWS - 1] * discount[ROWS - 1])[None, :]

    n = lax.axis_size("ctx")
    line = jax.ShapeDtypeStruct((1, ROWS), F32)
    values, local, records = local_call(
        values_kernel,
        [stats, critic_bias, reward[None, :], discount[None, :], matrix, tail, edge],
        "vsvvvvv",
        [line, line, jax.ShapeDtypeStruct((n, HD), F32)],
        "values",
        2 * ROWS * ROWS,
        MIB,
    )
    records = lax.all_to_all(records, "ctx", 0, 0, tiled=True)
    advantages = local_call(
        advantages_kernel,
        [index.astype(jnp.int32)[None], records, local, tail, edge],
        "svvvv",
        line,
        "advantages",
        ROWS,
        MIB,
    )
    return (residual_stream, values[0], advantages[0])


def solution(mesh):
    in_specs = (
        P("ctx", "tp"),
        P(),
        P("ctx", "tp"),
        P("ctx", "tp"),
        P("ctx", "tp"),
        P("tp"),
        P("tp"),
        P("tp"),
        P("tp", "ctx"),
        P("tp"),
        P("tp"),
        P(),
        P("ctx"),
        P("ctx"),
        P("ctx"),
    )
    out_specs = (P("ctx", "tp"), P("ctx"), P("ctx"))
    return jax.shard_map(
        on_device, mesh=mesh, in_specs=in_specs, out_specs=out_specs, check_vma=False
    )
```

```python
import math

import jax
import jax.numpy as jnp
from jax import lax
from jax.experimental import pallas as pl
from jax.experimental.pallas import tpu as pltpu
from jax.sharding import PartitionSpec as P

D = 5120
HD = 128
HALF = HD // 2
GROUP = 5
QW = GROUP * HD

EPS = 1e-06
GAMMA = 0.99
LAMBDA = 0.95
ROPE_BASE = 1000000.0
REWARD_SCALE = 0.25

X, Z, C, T = 4, 8, 2, 4
ROWS = 384
SHARD = 80
PIECE = D // T
MIB = 1 << 20

F32 = jnp.float32
BF16 = jnp.bfloat16


def place(x, z, c):
    return (x * Z + z) * C + c


def shift_tp(block, distance):
    return lax.ppermute(block, "tp", [(i, (i + distance) % T) for i in range(T)])


def local_call(kernel, operands, places, out_shape, name, flops, nbytes, scratch=(), mib=20):
    spaces = {"s": pltpu.SMEM, "v": pltpu.VMEM, "a": pl.ANY}
    return pl.pallas_call(
        kernel,
        in_specs=[pl.BlockSpec(memory_space=spaces[p]) for p in places],
        out_specs=jax.tree.map(lambda s: pl.BlockSpec(memory_space=pltpu.VMEM), out_shape),
        out_shape=out_shape,
        scratch_shapes=list(scratch),
        compiler_params=pltpu.CompilerParams(vmem_limit_bytes=mib * MIB),
        cost_estimate=pl.CostEstimate(flops=flops, bytes_accessed=nbytes, transcendentals=0),
        name=name,
    )(*operands)


def turned(u, cosine, sine):
    return u * cosine + pltpu.roll(u, HALF, 1) * sine


def norm_kernel(order, own, below, above, first, second, gain, normed_out):
    def squares(ref):
        x = ref[...].astype(F32)
        return jnp.sum(x * x, axis=-1, keepdims=True)

    half = first.shape[0]
    far = jnp.concatenate([squares(first), squares(second)], axis=0)
    mean = (squares(own) + squares(below) + squares(above) + far) / D
    scale = lax.rsqrt(mean + EPS)
    for at, ref in enumerate((own, below, above)):
        normed_out[at] = (ref[...].astype(F32) * scale * gain[order[at]]).astype(BF16)
    normed_out[T - 1, :half] = (first[...].astype(F32) * scale[:half] * gain[order[T - 1]]).astype(BF16)
    normed_out[T - 1, half:] = (second[...].astype(F32) * scale[half:] * gain[order[T - 1]]).astype(BF16)


def norm(order, pieces, gain):
    shape = jax.ShapeDtypeStruct((T, ROWS, PIECE), BF16)
    return local_call(norm_kernel, [order, *pieces, gain], "s" + "v" * 6, shape, "norm", 6 * ROWS * D, 4 * ROWS * D)


def project_kv_kernel(
    order, normed, w_own, w_other, bias, cosine, sine, key_out, value_out, mark_out, joined, sems
):
    core = order[T]
    copies = []
    for k in range(T):
        for at, (ref, lane) in enumerate(((w_own, core), (w_other, 1 - core))):
            copy = pltpu.make_async_copy(ref.at[order[k]], joined.at[k, :, lane], sems.at[k, at])
            copy.start()
            copies.append(copy)
    total = jnp.zeros((ROWS, 2 * HD), F32)
    for k in range(T):
        copies[2 * k].wait()
        copies[2 * k + 1].wait()
        total += jnp.dot(normed[k], joined[k].reshape(PIECE, 2 * HD), preferred_element_type=F32)
    key = turned(total[:, :HD] + bias[:, :HD], cosine[...], sine[...]).astype(BF16)
    value = (total[:, HD:] + bias[:, HD:]).astype(BF16)
    key_out[...] = key
    value_out[...] = value
    mark_out[...] = jnp.zeros_like(mark_out)


def project_kv(order, normed, w_own, w_other, bias, cosine, sine):
    one = jax.ShapeDtypeStruct((ROWS, HD), BF16)
    return local_call(
        project_kv_kernel,
        [order, normed, w_own, w_other, bias, cosine, sine],
        "svaavvv",
        [one, one, jax.ShapeDtypeStruct((1, ROWS), jnp.int32)],
        "project_kv",
        4 * ROWS * D * HD,
        2 * D * (2 * HD + ROWS),
        [pltpu.VMEM((T, Z, C, SHARD, 2 * HD), BF16), pltpu.SemaphoreType.DMA((T, 2))],
    )


def attend_kernel(
    order, index, normed, w, cosine, sine, mine, other, key, value, query_bias,
    top, bottom, pieces, held, acc, angles, seen, bias, sems, piece_sems, angle_sems, seen_sems,
):
    core = order[T]
    members = Z * C // 2
    stream = []
    for k in range(T):
        stream.append(pltpu.make_async_copy(normed.at[k], pieces.at[k], piece_sems.at[k]))
        for part in range(2):
            source = w.at[pl.ds(order[k] * Z * C + part * members, members), 1]
            stream.append(pltpu.make_async_copy(source, held.at[k, pl.ds(part * members, members)], sems.at[k, part]))
    stream += [pltpu.make_async_copy(ref, angles.at[at], angle_sems.at[at]) for at, ref in enumerate((cosine, sine))]
    near, far = pl.ds(ROWS, ROWS), pl.ds(0, ROWS)
    for at, (ref, lane, rows) in enumerate(((mine, core, far), (other, 1 - core, far), (key, 0, near), (value, 1, near))):
        stream.append(pltpu.make_async_copy(ref, seen.at[lane, rows], seen_sems.at[at]))
    ahead = 9
    for copy in stream[:ahead]:
        copy.start()
    row = lax.broadcasted_iota(jnp.int32, (ROWS, ROWS), 0)
    col = lax.broadcasted_iota(jnp.int32, (ROWS, ROWS), 1)
    bias[:, :ROWS] = jnp.where(jnp.full((ROWS, ROWS), index[0], jnp.int32) > 0, 0.0, -jnp.inf)
    bias[:, ROWS:] = jnp.where(row >= col, 0.0, -jnp.inf)
    for at, copy in enumerate(stream):
        copy.wait()
        if at + ahead < len(stream):
            stream[at + ahead].start()
        k = at // 3
        if at % 3 == 2 and k < T:
            part = jnp.dot(pieces[k], held[k].reshape(PIECE, QW), preferred_element_type=F32)
            acc[...] = part if k == 0 else acc[...] + part
    for head in range(GROUP):
        span = slice(head * HD, (head + 1) * HD)
        query = turned(acc[:, span] + query_bias[:, span], angles[0], angles[1]).astype(BF16)
        scores = lax.dot_general(query, seen[0], (((1,), (1,)), ((), ())), preferred_element_type=F32)
        scores = scores + bias[...]
        peak = jnp.max(scores, axis=-1, keepdims=True)
        weights = jnp.exp2((scores - peak) * (HD**-0.5 * math.log2(math.e)))
        total = jnp.sum(weights, axis=-1, keepdims=True)
        mixed = jnp.dot(weights.astype(BF16), seen[1], preferred_element_type=F32)
        mixed = (mixed / total).astype(BF16)
        top[:, span], bottom[:, span] = mixed[: ROWS // 2], mixed[ROWS // 2 :]


def attend(order, index, normed, w, cosine, sine, mine, other, key, value, query_bias):
    half = jax.ShapeDtypeStruct((ROWS // 2, QW), BF16)
    return local_call(
        attend_kernel,
        [order, index, normed, w, cosine, sine, mine, other, key, value, query_bias],
        "ssaaaaaaaav",
        [half, half],
        "attend",
        2 * ROWS * D * QW + 4 * ROWS * 2 * ROWS * QW,
        2 * D * (QW + ROWS),
        [
            pltpu.VMEM((T, ROWS, PIECE), BF16),
            pltpu.VMEM((T, Z * C, SHARD, QW), BF16),
            pltpu.VMEM((ROWS, QW), F32),
            pltpu.VMEM((2, ROWS, HD), F32),
            pltpu.VMEM((2, 2 * ROWS, HD), BF16),
            pltpu.VMEM((ROWS, 2 * ROWS), F32),
            pltpu.SemaphoreType.DMA((T, 2)),
            pltpu.SemaphoreType.DMA((T,)),
            pltpu.SemaphoreType.DMA((2,)),
            pltpu.SemaphoreType.DMA((4,)),
        ],
        50,
    )


def times(a, w):
    return lax.dot_general(a, w, (((1,), (1,)), ((), ())), preferred_element_type=F32)


def stack_kernel(first, second, out):
    out[0] = first[...]
    out[1] = second[...]


def joined(top, bottom):
    return jnp.concatenate([top[...], bottom[...]], axis=0)


def out_own_kernel(order, top, bottom, w, out, *refs):
    targets, sems = [refs[-2], *refs[:-2]], refs[-1]
    members = Z * C
    copies = [
        pltpu.make_async_copy(w.at[pl.ds(lax.rem(order[at] + 2, X) * members, members), 0], target, sems.at[at])
        for at, target in enumerate(targets)
    ]
    copies[0].start()
    copies[1].start()
    copies[0].wait()
    copies[2].start()
    copies[3].start()
    out[...] = times(joined(top, bottom), targets[0][...].reshape(PIECE, QW))
    for copy in copies[1:]:
        copy.wait()


def out_next_kernel(total, below_top, below_bottom, above_top, above_bottom, w_below, w_above, out):
    some = total[...] + times(joined(below_top, below_bottom), w_below[...].reshape(PIECE, QW))
    out[...] = some + times(joined(above_top, above_bottom), w_above[...].reshape(PIECE, QW))


def out_last_kernel(tokens, total, top, bottom, w, gain, head, resid_out, stats_out):
    lane = lax.broadcasted_iota(jnp.int32, (ROWS, HD), 1)
    resid = tokens[...].astype(F32) + total[...] + times(joined(top, bottom), w[...].reshape(PIECE, QW))
    resid_out[...] = resid.astype(BF16)
    squares = jnp.sum(resid * resid, axis=-1, keepdims=True)
    products = jnp.sum(resid * gain[...] * head[...], axis=-1, keepdims=True)
    both = jnp.where(lane == 0, squares, products).T[:8, :]
    for at in range(T):
        stats_out[at] = both


def values_kernel(stats, critic_bias, reward, discount, matrix, tail, edge, values_out, local_out, records_out):
    sums = stats[0] + stats[1] + stats[2] + stats[3]
    values = sums[1:2] * lax.rsqrt(sums[0:1] / D + EPS) + critic_bias[0]
    lane = lax.broadcasted_iota(jnp.int32, (1, ROWS), 1)
    following = jnp.where(lane == ROWS - 1, 0.0, pltpu.roll(values, ROWS - 1, 1))
    delta = reward[...] + discount[...] * following - values
    local = lax.dot_general(
        jnp.broadcast_to(delta, (8, ROWS)),
        matrix[...],
        (((1,), (1,)), ((), ())),
        precision=lax.Precision.HIGHEST,
        preferred_element_type=F32,
    )[0:1]
    values_out[...] = values
    local_out[...] = local
    head = lane[:, :HD] == 0
    record = jnp.zeros((1, HD), F32)
    for at, row in enumerate((values, local, tail[...], edge[...])):
        first = jnp.sum(jnp.where(head, row[:, :HD], 0.0), axis=-1, keepdims=True)
        record = jnp.where(lane[:, :HD] == at, first, record)
    records_out[...] = jnp.broadcast_to(record, records_out.shape)


def advantages_kernel(index, records, local, tail, edge, out):
    n = records.shape[0]
    row = lax.broadcasted_iota(jnp.int32, (n, HD), 0)

    def column(at):
        return jnp.broadcast_to(records[:, at : at + 1], (n, HD))

    def later(x, distance, fill):
        return jnp.where(row < n - distance, pltpu.roll(x, n - distance, 0), fill)

    first = column(0)
    term = column(1) + column(3) * later(first, 1, 0.0)
    decay = column(2)
    distance = 1
    while distance < n:
        term = term + decay * later(term, distance, 0.0)
        decay = decay * later(decay, distance, 1.0)
        distance *= 2
    after = row == index[0] + 1
    carry = jnp.sum(jnp.where(after, term, 0.0), axis=0, keepdims=True)
    value = jnp.sum(jnp.where(after, first, 0.0), axis=0, keepdims=True)
    for at in range(0, ROWS, HD):
        span = slice(at, at + HD)
        out[:, span] = local[:, span] + edge[:, span] * value + tail[:, span] * carry


def gather_by_all_to_all(block, axis, groups, n):
    everywhere = jnp.broadcast_to(block[None], (n, *block.shape))
    return lax.all_to_all(everywhere, axis, 0, 0, axis_index_groups=groups)


Z_GROUPS = [[place(x, z, c) for z in range(Z)] for x in range(X) for c in range(C)]
X_GROUPS = [[place(x, z, c) for x in range(X)] for z in range(Z) for c in range(C)]


def other_core(block):
    return lax.ppermute(block, "ctx", [(i, i ^ 1) for i in range(X * Z * C)])


OVER_X = ((1, 0), (3, 0), (2, 0))
OVER_Z = ((0, 2), (0, 6), (0, 4))
LAST = ((0, 1),)
TREES = ((OVER_X, OVER_Z, LAST), (OVER_Z, OVER_X, LAST))


def broadcast_anchor(key, value):
    here = lax.axis_index("ctx")
    x, z, core = here // (Z * C), here // C % Z, here % C
    block = jnp.where(core == 0, key, lax.ppermute(value, "ctx", [(0, 1)]))
    holders = [[(0, 0)], [(0, 0)]]
    for stages in zip(*TREES):
        holding = jnp.zeros((), jnp.bool_)
        for c in range(C):
            xs, zs = ({h[axis] for h in holders[c]} for axis in range(2))
            among = lambda at, seen: sum((at == v).astype(jnp.int32) for v in seen) > 0
            holding |= (core == c) & among(x, sorted(xs)) & among(z, sorted(zs))
        sent = None
        fresh = [[], []]
        for shifts in zip(*stages):
            pairs = []
            for c, (dx, dz) in enumerate(shifts):
                targets = [((px + dx) % X, (pz + dz) % Z) for px, pz in holders[c]]
                pairs += [(place(*a, c), place(*b, c)) for a, b in zip(holders[c], targets)]
                fresh[c] += targets
            got = lax.ppermute(block, "ctx", pairs)
            sent = got if sent is None else sent + got
        block = jnp.where(holding, block, sent)
        holders = [old + new for old, new in zip(holders, fresh)]
    return block, other_core(block)


def on_device(
    tokens,
    input_gain,
    w_query,
    w_key,
    w_value,
    query_bias,
    key_bias,
    value_bias,
    w_out,
    final_gain,
    critic_head,
    critic_bias,
    rewards,
    turn_ends,
    episode_done,
):
    index = lax.axis_index("ctx")
    mine = lax.axis_index("tp")
    order = jnp.stack([mine, (mine + 3) % T, (mine + 1) % T, (mine + 2) % T, index % C]).astype(jnp.int32)

    corner = [
        (place(x, z, c) * T + y, place((y + 2) % X, z, c) * T + x)
        for x in range(X)
        for z in range(Z)
        for c in range(C)
        for y in range(T)
    ]
    out_block = lax.ppermute(w_out.T, ("ctx", "tp"), corner)
    both = local_call(
        stack_kernel, [out_block, w_query], "vv", jax.ShapeDtypeStruct((2, SHARD, QW), BF16), "stack", 0, 8 * SHARD * QW
    )
    weights = lax.all_gather(both, "ctx")

    half = ROWS // 2
    below, above = shift_tp(tokens, 1), shift_tp(tokens, -1)
    kv_part = gather_by_all_to_all(jnp.concatenate([w_key, w_value], axis=1), "ctx", Z_GROUPS, Z)
    below, above, kv_part = lax.optimization_barrier((below, above, kv_part))
    first, second = shift_tp(below[:half], 1), shift_tp(above[half:], -1)
    kv_own = gather_by_all_to_all(kv_part, "ctx", X_GROUPS, X)
    first, second, kv_own = lax.optimization_barrier((first, second, kv_own))
    normed = norm(order, (tokens, below, above, first, second), input_gain.reshape(T, 1, PIECE))
    kv_other = other_core(kv_own)
    positions = (index * ROWS + jnp.arange(ROWS)).astype(F32)
    steps = jnp.arange(HALF).astype(F32)
    inverse = 1.0 / ROPE_BASE ** (steps * 2.0 / HD)
    angle = positions[:, None] * inverse[None, :]
    cosine, sine = jnp.cos(angle), jnp.sin(angle)
    cosine = jnp.concatenate([cosine, cosine], axis=1)
    sine = jnp.concatenate([-sine, sine], axis=1)
    kv_bias = jnp.concatenate([key_bias, value_bias])[None, :]
    key, value, mark = project_kv(order, normed, kv_own, kv_other, kv_bias, cosine, sine)
    turn_ends, episode_done = turn_ends + mark[0], episode_done + mark[0]
    ends = jnp.maximum(turn_ends, episode_done)
    discount = jnp.where(ends > 0, GAMMA, 1.0).astype(F32) * (1 - episode_done).astype(F32)
    reward = REWARD_SCALE * (rewards * ends).astype(F32)
    decaying = ends * (1 - episode_done)
    zero_int = jnp.zeros((1,), jnp.int32)
    decay_count = jnp.concatenate([zero_int, jnp.cumsum(decaying)])
    done_count = jnp.concatenate([zero_int, jnp.cumsum(episode_done)])
    rate = GAMMA * LAMBDA
    later = jnp.arange(ROWS)[None, :] >= jnp.arange(ROWS)[:, None]
    same_episode = done_count[None, :ROWS] == done_count[:ROWS, None]
    powers = (decay_count[None, :ROWS] - decay_count[:ROWS, None]).astype(F32)
    matrix = jnp.where(later & same_episode, jnp.power(rate, powers), 0.0)
    tail_powers = (decay_count[ROWS] - decay_count[:ROWS]).astype(F32)
    tail = jnp.where(done_count[ROWS] == done_count[:ROWS], jnp.power(rate, tail_powers), 0.0)[None, :]
    edge = (matrix[:, ROWS - 1] * discount[ROWS - 1])[None, :]

    held, sent = broadcast_anchor(key, value)
    sent, tail, edge = lax.optimization_barrier((sent, tail, edge))
    index_ref = index.astype(jnp.int32)[None]
    top, bottom = attend(order, index_ref, normed, weights, cosine, sine, held, sent, key, value, query_bias[None, :])

    below_top, above_bottom = shift_tp(top, 1), shift_tp(bottom, -1)
    below_bottom, above_top = shift_tp(bottom, 1), shift_tp(top, -1)
    flops = 2 * ROWS * QW * PIECE
    wide = jax.ShapeDtypeStruct((ROWS, PIECE), F32)
    group = jax.ShapeDtypeStruct((Z * C, SHARD, QW), BF16)
    total, w_below, w_above, w_far = local_call(
        out_own_kernel,
        [order, top, bottom, weights],
        "svva",
        [wide, group, group, group],
        "out_own",
        flops,
        8 * MIB,
        [pltpu.VMEM(group.shape, BF16), pltpu.SemaphoreType.DMA((T,))],
        42,
    )
    total, below_top = lax.optimization_barrier((total, below_top))
    far_top, far_bottom = shift_tp(below_top, 1), shift_tp(above_bottom, -1)
    total = local_call(
        out_next_kernel,
        [total, below_top, below_bottom, above_top, above_bottom, w_below, w_above],
        "vvvvvvv",
        wide,
        "out_next",
        2 * flops,
        6 * MIB,
    )
    residual_stream, stats = local_call(
        out_last_kernel,
        [tokens, total, far_top, far_bottom, w_far, final_gain[None, :], critic_head[None, :]],
        "vvvvvvv",
        [jax.ShapeDtypeStruct((ROWS, PIECE), BF16), jax.ShapeDtypeStruct((T, 8, ROWS), F32)],
        "out_last",
        flops,
        6 * MIB,
    )
    stats = lax.all_to_all(stats, "tp", 0, 0)

    n = lax.axis_size("ctx")
    line = jax.ShapeDtypeStruct((1, ROWS), F32)
    values, local, records = local_call(
        values_kernel,
        [stats, critic_bias, reward[None, :], discount[None, :], matrix, tail, edge],
        "vsvvvvv",
        [line, line, jax.ShapeDtypeStruct((n, HD), F32)],
        "values",
        2 * ROWS * ROWS,
        MIB,
    )
    records = lax.all_to_all(records, "ctx", 0, 0, tiled=True)
    advantages = local_call(
        advantages_kernel,
        [index.astype(jnp.int32)[None], records, local, tail, edge],
        "svvvv",
        line,
        "advantages",
        ROWS,
        MIB,
    )
    return (residual_stream, values[0], advantages[0])


def solution(mesh):
    in_specs = (
        P("ctx", "tp"),
        P(),
        P("ctx", "tp"),
        P("ctx", "tp"),
        P("ctx", "tp"),
        P("tp"),
        P("tp"),
        P("tp"),
        P("tp", "ctx"),
        P("tp"),
        P("tp"),
        P(),
        P("ctx"),
        P("ctx"),
        P("ctx"),
    )
    out_specs = (P("ctx", "tp"), P("ctx"), P("ctx"))
    return jax.shard_map(
        on_device, mesh=mesh, in_specs=in_specs, out_specs=out_specs, check_vma=False
    )
```

```python
import math

import jax
import jax.numpy as jnp
from jax import lax
from jax.experimental import pallas as pl
from jax.experimental.pallas import tpu as pltpu
from jax.sharding import PartitionSpec as P

D = 5120
HD = 128
HALF = HD // 2
GROUP = 5
QW = GROUP * HD

EPS = 1e-06
GAMMA = 0.99
LAMBDA = 0.95
ROPE_BASE = 1000000.0
REWARD_SCALE = 0.25

X, Z, C, T = 4, 8, 2, 4
ROWS = 384
SHARD = 80
PIECE = D // T
MIB = 1 << 20

F32 = jnp.float32
BF16 = jnp.bfloat16


def place(x, z, c):
    return (x * Z + z) * C + c


def shift_tp(block, distance):
    return lax.ppermute(block, "tp", [(i, (i + distance) % T) for i in range(T)])


def local_call(kernel, operands, places, out_shape, name, flops, nbytes, scratch=(), mib=20):
    spaces = {"s": pltpu.SMEM, "v": pltpu.VMEM, "a": pl.ANY}
    return pl.pallas_call(
        kernel,
        in_specs=[pl.BlockSpec(memory_space=spaces[p]) for p in places],
        out_specs=jax.tree.map(lambda s: pl.BlockSpec(memory_space=pltpu.VMEM), out_shape),
        out_shape=out_shape,
        scratch_shapes=list(scratch),
        compiler_params=pltpu.CompilerParams(vmem_limit_bytes=mib * MIB),
        cost_estimate=pl.CostEstimate(flops=flops, bytes_accessed=nbytes, transcendentals=0),
        name=name,
    )(*operands)


def turned(u, cosine, sine):
    return u * cosine + pltpu.roll(u, HALF, 1) * sine


def norm_kernel(order, own, below, above, first, second, gain, normed_out):
    def squares(ref):
        x = ref[...].astype(F32)
        return jnp.sum(x * x, axis=-1, keepdims=True)

    half = first.shape[0]
    far = jnp.concatenate([squares(first), squares(second)], axis=0)
    mean = (squares(own) + squares(below) + squares(above) + far) / D
    scale = lax.rsqrt(mean + EPS)
    for at, ref in enumerate((own, below, above)):
        normed_out[at] = (ref[...].astype(F32) * scale * gain[order[at]]).astype(BF16)
    normed_out[T - 1, :half] = (first[...].astype(F32) * scale[:half] * gain[order[T - 1]]).astype(BF16)
    normed_out[T - 1, half:] = (second[...].astype(F32) * scale[half:] * gain[order[T - 1]]).astype(BF16)


def norm(order, pieces, gain):
    shape = jax.ShapeDtypeStruct((T, ROWS, PIECE), BF16)
    return local_call(norm_kernel, [order, *pieces, gain], "s" + "v" * 6, shape, "norm", 6 * ROWS * D, 4 * ROWS * D)


def project_kv_kernel(
    order, normed, w_own, w_other, bias, cosine, sine, key_out, value_out, mark_out, joined, sems
):
    core = order[T]
    copies = []
    for k in range(T):
        for at, (ref, lane) in enumerate(((w_own, core), (w_other, 1 - core))):
            copy = pltpu.make_async_copy(ref.at[order[k]], joined.at[k, :, lane], sems.at[k, at])
            copy.start()
            copies.append(copy)
    total = jnp.zeros((ROWS, 2 * HD), F32)
    for k in range(T):
        copies[2 * k].wait()
        copies[2 * k + 1].wait()
        total += jnp.dot(normed[k], joined[k].reshape(PIECE, 2 * HD), preferred_element_type=F32)
    key = turned(total[:, :HD] + bias[:, :HD], cosine[...], sine[...]).astype(BF16)
    value = (total[:, HD:] + bias[:, HD:]).astype(BF16)
    key_out[...] = key
    value_out[...] = value
    mark_out[...] = jnp.zeros_like(mark_out)


def project_kv(order, normed, w_own, w_other, bias, cosine, sine):
    one = jax.ShapeDtypeStruct((ROWS, HD), BF16)
    return local_call(
        project_kv_kernel,
        [order, normed, w_own, w_other, bias, cosine, sine],
        "svaavvv",
        [one, one, jax.ShapeDtypeStruct((1, ROWS), jnp.int32)],
        "project_kv",
        4 * ROWS * D * HD,
        2 * D * (2 * HD + ROWS),
        [pltpu.VMEM((T, Z, C, SHARD, 2 * HD), BF16), pltpu.SemaphoreType.DMA((T, 2))],
    )


def attend_kernel(
    order, index, normed, w, cosine, sine, mine, other, key, value, query_bias,
    top, bottom, pieces, held, acc, angles, seen, bias, sems, piece_sems, angle_sems, seen_sems,
):
    core = order[T]
    members = Z * C // 2
    stream = []
    for k in range(T):
        stream.append(pltpu.make_async_copy(normed.at[k], pieces.at[k], piece_sems.at[k]))
        for part in range(2):
            source = w.at[pl.ds(order[k] * Z * C + part * members, members), 1]
            stream.append(pltpu.make_async_copy(source, held.at[k, pl.ds(part * members, members)], sems.at[k, part]))
    stream += [pltpu.make_async_copy(ref, angles.at[at], angle_sems.at[at]) for at, ref in enumerate((cosine, sine))]
    near, far = pl.ds(ROWS, ROWS), pl.ds(0, ROWS)
    for at, (ref, lane, rows) in enumerate(((mine, core, far), (other, 1 - core, far), (key, 0, near), (value, 1, near))):
        stream.append(pltpu.make_async_copy(ref, seen.at[lane, rows], seen_sems.at[at]))
    ahead = 9
    for copy in stream[:ahead]:
        copy.start()
    row = lax.broadcasted_iota(jnp.int32, (ROWS, ROWS), 0)
    col = lax.broadcasted_iota(jnp.int32, (ROWS, ROWS), 1)
    bias[:, :ROWS] = jnp.where(jnp.full((ROWS, ROWS), index[0], jnp.int32) > 0, 0.0, -jnp.inf)
    bias[:, ROWS:] = jnp.where(row >= col, 0.0, -jnp.inf)
    for at, copy in enumerate(stream):
        copy.wait()
        if at + ahead < len(stream):
            stream[at + ahead].start()
        k = at // 3
        if at % 3 == 2 and k < T:
            part = jnp.dot(pieces[k], held[k].reshape(PIECE, QW), preferred_element_type=F32)
            acc[...] = part if k == 0 else acc[...] + part
    for head in range(GROUP):
        span = slice(head * HD, (head + 1) * HD)
        query = turned(acc[:, span] + query_bias[:, span], angles[0], angles[1]).astype(BF16)
        scores = lax.dot_general(query, seen[0], (((1,), (1,)), ((), ())), preferred_element_type=F32)
        scores = scores + bias[...]
        peak = jnp.max(scores, axis=-1, keepdims=True)
        weights = jnp.exp2((scores - peak) * (HD**-0.5 * math.log2(math.e)))
        total = jnp.sum(weights, axis=-1, keepdims=True)
        mixed = jnp.dot(weights.astype(BF16), seen[1], preferred_element_type=F32)
        mixed = (mixed / total).astype(BF16)
        top[:, span], bottom[:, span] = mixed[: ROWS // 2], mixed[ROWS // 2 :]


def attend(order, index, normed, w, cosine, sine, mine, other, key, value, query_bias):
    half = jax.ShapeDtypeStruct((ROWS // 2, QW), BF16)
    return local_call(
        attend_kernel,
        [order, index, normed, w, cosine, sine, mine, other, key, value, query_bias],
        "ssaaaaaaaav",
        [half, half],
        "attend",
        2 * ROWS * D * QW + 4 * ROWS * 2 * ROWS * QW,
        2 * D * (QW + ROWS),
        [
            pltpu.VMEM((T, ROWS, PIECE), BF16),
            pltpu.VMEM((T, Z * C, SHARD, QW), BF16),
            pltpu.VMEM((ROWS, QW), F32),
            pltpu.VMEM((2, ROWS, HD), F32),
            pltpu.VMEM((2, 2 * ROWS, HD), BF16),
            pltpu.VMEM((ROWS, 2 * ROWS), F32),
            pltpu.SemaphoreType.DMA((T, 2)),
            pltpu.SemaphoreType.DMA((T,)),
            pltpu.SemaphoreType.DMA((2,)),
            pltpu.SemaphoreType.DMA((4,)),
        ],
        50,
    )


def times(a, w):
    return lax.dot_general(a, w, (((1,), (1,)), ((), ())), preferred_element_type=F32)


def stack_kernel(first, second, out):
    out[0] = first[...]
    out[1] = second[...]


def joined(top, bottom):
    return jnp.concatenate([top[...], bottom[...]], axis=0)


def out_own_kernel(order, top, bottom, w, out, *refs):
    targets, sems = [refs[-2], *refs[:-2]], refs[-1]
    members = Z * C
    copies = [
        pltpu.make_async_copy(w.at[pl.ds(lax.rem(order[at] + 2, X) * members, members), 0], target, sems.at[at])
        for at, target in enumerate(targets)
    ]
    copies[0].start()
    copies[1].start()
    copies[0].wait()
    copies[2].start()
    copies[3].start()
    out[...] = times(joined(top, bottom), targets[0][...].reshape(PIECE, QW))
    for copy in copies[1:]:
        copy.wait()


def out_next_kernel(total, below_top, below_bottom, above_top, above_bottom, w_below, w_above, out):
    some = total[...] + times(joined(below_top, below_bottom), w_below[...].reshape(PIECE, QW))
    out[...] = some + times(joined(above_top, above_bottom), w_above[...].reshape(PIECE, QW))


def out_last_kernel(tokens, total, top, bottom, w, gain, head, resid_out, stats_out):
    lane = lax.broadcasted_iota(jnp.int32, (ROWS, HD), 1)
    resid = tokens[...].astype(F32) + total[...] + times(joined(top, bottom), w[...].reshape(PIECE, QW))
    resid_out[...] = resid.astype(BF16)
    squares = jnp.sum(resid * resid, axis=-1, keepdims=True)
    products = jnp.sum(resid * gain[...] * head[...], axis=-1, keepdims=True)
    both = jnp.where(lane == 0, squares, products).T[:2, :]
    for at in range(T):
        stats_out[at] = both


def values_kernel(stats, critic_bias, reward, discount, matrix, tail, edge, values_out, local_out, records_out):
    sums = stats[0] + stats[1] + stats[2] + stats[3]
    values = sums[1:2] * lax.rsqrt(sums[0:1] / D + EPS) + critic_bias[0]
    lane = lax.broadcasted_iota(jnp.int32, (1, ROWS), 1)
    following = jnp.where(lane == ROWS - 1, 0.0, pltpu.roll(values, ROWS - 1, 1))
    delta = reward[...] + discount[...] * following - values
    local = lax.dot_general(
        jnp.broadcast_to(delta, (8, ROWS)),
        matrix[...],
        (((1,), (1,)), ((), ())),
        precision=lax.Precision.HIGHEST,
        preferred_element_type=F32,
    )[0:1]
    values_out[...] = values
    local_out[...] = local
    head = lane[:, :HD] == 0
    record = jnp.zeros((1, HD), F32)
    for at, row in enumerate((values, local, tail[...], edge[...])):
        first = jnp.sum(jnp.where(head, row[:, :HD], 0.0), axis=-1, keepdims=True)
        record = jnp.where(lane[:, :HD] == at, first, record)
    records_out[...] = jnp.broadcast_to(record, records_out.shape)


def advantages_kernel(index, records, local, tail, edge, out):
    n = records.shape[0]
    row = lax.broadcasted_iota(jnp.int32, (n, HD), 0)

    def column(at):
        return jnp.broadcast_to(records[:, at : at + 1], (n, HD))

    def later(x, distance, fill):
        return jnp.where(row < n - distance, pltpu.roll(x, n - distance, 0), fill)

    first = column(0)
    term = column(1) + column(3) * later(first, 1, 0.0)
    decay = column(2)
    distance = 1
    while distance < n:
        term = term + decay * later(term, distance, 0.0)
        decay = decay * later(decay, distance, 1.0)
        distance *= 2
    after = row == index[0] + 1
    carry = jnp.sum(jnp.where(after, term, 0.0), axis=0, keepdims=True)
    value = jnp.sum(jnp.where(after, first, 0.0), axis=0, keepdims=True)
    for at in range(0, ROWS, HD):
        span = slice(at, at + HD)
        out[:, span] = local[:, span] + edge[:, span] * value + tail[:, span] * carry


def gather_by_all_to_all(block, axis, groups, n):
    everywhere = jnp.broadcast_to(block[None], (n, *block.shape))
    return lax.all_to_all(everywhere, axis, 0, 0, axis_index_groups=groups)


Z_GROUPS = [[place(x, z, c) for z in range(Z)] for x in range(X) for c in range(C)]
X_GROUPS = [[place(x, z, c) for x in range(X)] for z in range(Z) for c in range(C)]


def other_core(block):
    return lax.ppermute(block, "ctx", [(i, i ^ 1) for i in range(X * Z * C)])


OVER_X = ((1, 0), (3, 0), (2, 0))
OVER_Z = ((0, 2), (0, 6), (0, 4))
LAST = ((0, 1),)
TREES = ((OVER_X, OVER_Z, LAST), (OVER_Z, OVER_X, LAST))


def broadcast_anchor(key, value):
    here = lax.axis_index("ctx")
    x, z, core = here // (Z * C), here // C % Z, here % C
    block = jnp.where(core == 0, key, lax.ppermute(value, "ctx", [(0, 1)]))
    holders = [[(0, 0)], [(0, 0)]]
    for stages in zip(*TREES):
        holding = jnp.zeros((), jnp.bool_)
        for c in range(C):
            xs, zs = ({h[axis] for h in holders[c]} for axis in range(2))
            among = lambda at, seen: sum((at == v).astype(jnp.int32) for v in seen) > 0
            holding |= (core == c) & among(x, sorted(xs)) & among(z, sorted(zs))
        sent = None
        fresh = [[], []]
        for shifts in zip(*stages):
            pairs = []
            for c, (dx, dz) in enumerate(shifts):
                targets = [((px + dx) % X, (pz + dz) % Z) for px, pz in holders[c]]
                pairs += [(place(*a, c), place(*b, c)) for a, b in zip(holders[c], targets)]
                fresh[c] += targets
            got = lax.ppermute(block, "ctx", pairs)
            sent = got if sent is None else sent + got
        block = jnp.where(holding, block, sent)
        holders = [old + new for old, new in zip(holders, fresh)]
    return block, other_core(block)


def on_device(
    tokens,
    input_gain,
    w_query,
    w_key,
    w_value,
    query_bias,
    key_bias,
    value_bias,
    w_out,
    final_gain,
    critic_head,
    critic_bias,
    rewards,
    turn_ends,
    episode_done,
):
    index = lax.axis_index("ctx")
    mine = lax.axis_index("tp")
    order = jnp.stack([mine, (mine + 3) % T, (mine + 1) % T, (mine + 2) % T, index % C]).astype(jnp.int32)

    corner = [
        (place(x, z, c) * T + y, place((y + 2) % X, z, c) * T + x)
        for x in range(X)
        for z in range(Z)
        for c in range(C)
        for y in range(T)
    ]
    out_block = lax.ppermute(w_out.T, ("ctx", "tp"), corner)
    both = local_call(
        stack_kernel, [out_block, w_query], "vv", jax.ShapeDtypeStruct((2, SHARD, QW), BF16), "stack", 0, 8 * SHARD * QW
    )
    weights = lax.all_gather(both, "ctx")

    half = ROWS // 2
    below, above = shift_tp(tokens, 1), shift_tp(tokens, -1)
    kv_part = gather_by_all_to_all(jnp.concatenate([w_key, w_value], axis=1), "ctx", Z_GROUPS, Z)
    below, above, kv_part = lax.optimization_barrier((below, above, kv_part))
    first, second = shift_tp(below[:half], 1), shift_tp(above[half:], -1)
    kv_own = gather_by_all_to_all(kv_part, "ctx", X_GROUPS, X)
    first, second, kv_own = lax.optimization_barrier((first, second, kv_own))
    normed = norm(order, (tokens, below, above, first, second), input_gain.reshape(T, 1, PIECE))
    kv_other = other_core(kv_own)
    positions = (index * ROWS + jnp.arange(ROWS)).astype(F32)
    steps = jnp.arange(HALF).astype(F32)
    inverse = 1.0 / ROPE_BASE ** (steps * 2.0 / HD)
    angle = positions[:, None] * inverse[None, :]
    cosine, sine = jnp.cos(angle), jnp.sin(angle)
    cosine = jnp.concatenate([cosine, cosine], axis=1)
    sine = jnp.concatenate([-sine, sine], axis=1)
    kv_bias = jnp.concatenate([key_bias, value_bias])[None, :]
    key, value, mark = project_kv(order, normed, kv_own, kv_other, kv_bias, cosine, sine)
    turn_ends, episode_done = turn_ends + mark[0], episode_done + mark[0]
    ends = jnp.maximum(turn_ends, episode_done)
    discount = jnp.where(ends > 0, GAMMA, 1.0).astype(F32) * (1 - episode_done).astype(F32)
    reward = REWARD_SCALE * (rewards * ends).astype(F32)
    decaying = ends * (1 - episode_done)
    zero_int = jnp.zeros((1,), jnp.int32)
    decay_count = jnp.concatenate([zero_int, jnp.cumsum(decaying)])
    done_count = jnp.concatenate([zero_int, jnp.cumsum(episode_done)])
    rate = GAMMA * LAMBDA
    later = jnp.arange(ROWS)[None, :] >= jnp.arange(ROWS)[:, None]
    same_episode = done_count[None, :ROWS] == done_count[:ROWS, None]
    powers = (decay_count[None, :ROWS] - decay_count[:ROWS, None]).astype(F32)
    matrix = jnp.where(later & same_episode, jnp.power(rate, powers), 0.0)
    tail_powers = (decay_count[ROWS] - decay_count[:ROWS]).astype(F32)
    tail = jnp.where(done_count[ROWS] == done_count[:ROWS], jnp.power(rate, tail_powers), 0.0)[None, :]
    edge = (matrix[:, ROWS - 1] * discount[ROWS - 1])[None, :]

    held, sent = broadcast_anchor(key, value)
    sent, tail, edge = lax.optimization_barrier((sent, tail, edge))
    index_ref = index.astype(jnp.int32)[None]
    top, bottom = attend(order, index_ref, normed, weights, cosine, sine, held, sent, key, value, query_bias[None, :])

    below_top, above_bottom = shift_tp(top, 1), shift_tp(bottom, -1)
    below_bottom, above_top = shift_tp(bottom, 1), shift_tp(top, -1)
    flops = 2 * ROWS * QW * PIECE
    wide = jax.ShapeDtypeStruct((ROWS, PIECE), F32)
    group = jax.ShapeDtypeStruct((Z * C, SHARD, QW), BF16)
    total, w_below, w_above, w_far = local_call(
        out_own_kernel,
        [order, top, bottom, weights],
        "svva",
        [wide, group, group, group],
        "out_own",
        flops,
        8 * MIB,
        [pltpu.VMEM(group.shape, BF16), pltpu.SemaphoreType.DMA((T,))],
        42,
    )
    total, below_top = lax.optimization_barrier((total, below_top))
    far_top, far_bottom = shift_tp(below_top, 1), shift_tp(above_bottom, -1)
    total = local_call(
        out_next_kernel,
        [total, below_top, below_bottom, above_top, above_bottom, w_below, w_above],
        "vvvvvvv",
        wide,
        "out_next",
        2 * flops,
        6 * MIB,
    )
    residual_stream, stats = local_call(
        out_last_kernel,
        [tokens, total, far_top, far_bottom, w_far, final_gain[None, :], critic_head[None, :]],
        "vvvvvvv",
        [jax.ShapeDtypeStruct((ROWS, PIECE), BF16), jax.ShapeDtypeStruct((T, 2, ROWS), F32)],
        "out_last",
        flops,
        6 * MIB,
    )
    stats = lax.all_to_all(stats, "tp", 0, 0)

    n = lax.axis_size("ctx")
    line = jax.ShapeDtypeStruct((1, ROWS), F32)
    values, local, records = local_call(
        values_kernel,
        [stats, critic_bias, reward[None, :], discount[None, :], matrix, tail, edge],
        "vsvvvvv",
        [line, line, jax.ShapeDtypeStruct((n, HD), F32)],
        "values",
        2 * ROWS * ROWS,
        MIB,
    )
    records = lax.all_to_all(records, "ctx", 0, 0, tiled=True)
    advantages = local_call(
        advantages_kernel,
        [index.astype(jnp.int32)[None], records, local, tail, edge],
        "svvvv",
        line,
        "advantages",
        ROWS,
        MIB,
    )
    return (residual_stream, values[0], advantages[0])


def solution(mesh):
    in_specs = (
        P("ctx", "tp"),
        P(),
        P("ctx", "tp"),
        P("ctx", "tp"),
        P("ctx", "tp"),
        P("tp"),
        P("tp"),
        P("tp"),
        P("tp", "ctx"),
        P("tp"),
        P("tp"),
        P(),
        P("ctx"),
        P("ctx"),
        P("ctx"),
    )
    out_specs = (P("ctx", "tp"), P("ctx"), P("ctx"))
    return jax.shard_map(
        on_device, mesh=mesh, in_specs=in_specs, out_specs=out_specs, check_vma=False
    )
```
